256 devices in a mesh: space: 32 (over z, x), batch: 8 (over y, core).
Axes of the slice: x: 4, y: 4, z: 8, core: 2. Of those that a mesh axis runs over, the one named last changes fastest.
Arguments:
- cotangent: float32 [16, 192, 128, 384], P('batch', 'space'), may hold values from -6 to 6
- grid_state: bfloat16 [16, 256, 128, 512], P('batch', 'space'), may hold values from -6 to 6
- legendre: bfloat16 [192, 192, 256], P('space'), may hold values from -0.375 to 0.375
- inverse: float32 [192, 4, 32, 32], P('space'), may hold values from -1 to 1
- gauss_weights: float32 [256], replicated, may hold values from 0.5 to 1.5
- w_in: bfloat16 [128, 256], replicated, may hold values from -0.5 to 0.5
- bias_in: float32 [256], replicated, may hold values from -3 to 3
- w_mid: bfloat16 [256, 256], replicated, may hold values from -0.375 to 0.375
- bias_mid: float32 [256], replicated, may hold values from -3 to 3
- w_out: bfloat16 [256, 128], replicated, may hold values from -0.5 to 0.5
Outputs:
- grad_state: float32 [16, 192, 128, 384], P('batch', 'space')
- grad_w_in: float32 [128, 256], replicated
- grad_bias_in: float32 [256], replicated
- grad_w_mid: float32 [256, 256], replicated
- grad_bias_mid: float32 [256], replicated
- grad_w_out: float32 [256, 128], replicated
The draws below stay inside these ranges and needn't reach their ends.
All inputs are finite; a program needn't handle non-finite values.
Results may differ from the reference program's by a relative error of at most 0.0075.
Values may be sent and summed in bfloat16 or wider, within the bound.
A program may use at most 128 MiB of HBM per device.

```python
import math
import jax
import jax.numpy as jnp
from jax import lax

LEV = 32
F = 4
HID = 256
LON = 512
L = 192
CH = 128
M = 192
LAT = 256
B = 16


def shard_levels(key, extent, pieces, least, largest):
    factor_of = 1.0
    for dim, shards_of in pieces:
        draws = jax.random.uniform(jax.random.fold_in(jax.random.fold_in(key, 6), dim), (shards_of,), jnp.float32, least / len(pieces), largest / len(pieces))
        factor_of = factor_of * jnp.repeat(jnp.exp(draws), extent[dim] // shards_of).reshape((-1,) + (1,) * (len(extent) - 1 - dim))
    return factor_of


def noise(key, dims, spread, bound, split=(), kind=jnp.bfloat16):
    loudness = shard_levels(key, dims, split, -0.22, 0.18) if split else 1.0
    array = jax.random.normal(key, dims, jnp.float32) * spread * loudness
    return jnp.minimum(jnp.maximum(array, -bound), bound).astype(kind)


def setup_inputs(seed: int = 0) -> dict:
    splits = jax.random.split(jax.random.key(seed), 11)
    cotangent = noise(splits[0], (B, M, CH, 2 * L), 1.0, 6.0, ((0, 8), (1, 32)), jnp.float32)
    grid_state = noise(splits[1], (B, LAT, CH, LON), 1.0, 6.0, ((0, 8), (1, 32)))
    legendre = noise(splits[2], (M, L, LAT), LAT ** -0.5, 0.375, ((0, 32),))
    inverse = noise(splits[3], (M, F, LEV, LEV), LEV ** -0.5, 1.0, ((0, 32),), jnp.float32)
    gauss_weights = jnp.clip(jax.random.uniform(splits[4], (LAT,), jnp.float32, 0.5, 1.5), 0.5, 1.5)
    w_in = noise(splits[5], (CH, HID), CH ** -0.5, 0.5)
    bias_in = noise(splits[6], (HID,), 0.5, 3.0, (), jnp.float32)
    w_mid = noise(splits[7], (HID, HID), HID ** -0.5, 0.375)
    bias_mid = noise(splits[8], (HID,), 0.5, 3.0, (), jnp.float32)
    w_out = noise(splits[9], (HID, CH), CH ** -0.5, 0.5)
    return dict(cotangent=cotangent, grid_state=grid_state, legendre=legendre, inverse=inverse, gauss_weights=gauss_weights, w_in=w_in, bias_in=bias_in, w_mid=w_mid, bias_mid=bias_mid, w_out=w_out)


HIGH = lax.Precision.HIGHEST

def fourier_table(waves, longitudes):
    wave_ids = jnp.arange(waves, dtype=jnp.int32)[:, None]
    columns = jnp.arange(longitudes, dtype=jnp.int32)[None, :]
    phase = (wave_ids * columns % longitudes).astype(jnp.float32) * (2.0 * math.pi / longitudes)
    scale = 1.0 / math.sqrt(waves)
    return jnp.stack([jnp.cos(phase) * scale, -jnp.sin(phase) * scale]).astype(jnp.bfloat16)

def gelu_value(v):
    inner = 0.7978845608 * (v + 0.044715 * v * v * v)
    return 0.5 * v * (1.0 + jnp.tanh(inner))

def gelu_slope(v):
    tanh_part = jnp.tanh(0.7978845608 * (v + 0.044715 * v * v * v))
    return 0.5 * (1.0 + tanh_part) + 0.5 * v * (1.0 - tanh_part * tanh_part) * 0.7978845608 * (1.0 + 0.134145 * v * v)

def reference(cotangent, grid_state, legendre, inverse, gauss_weights, w_in, bias_in, w_mid, bias_mid, w_out):
    table = fourier_table(M, LON).astype(jnp.float32)
    legendre_wide = legendre.astype(jnp.float32)
    w_in_wide = w_in.astype(jnp.float32)
    w_mid_wide = w_mid.astype(jnp.float32)
    w_out_wide = w_out.astype(jnp.float32)

    def one_state(pair):
        cot_one, grid_one = pair
        cot_fields = cot_one.reshape(M, F, LEV, 2 * L)
        spec_grad = jnp.einsum('mfjk,mfjl->mfkl', inverse, cot_fields, precision=HIGH).reshape(M, CH, 2 * L)
        spec_half = spec_grad.astype(jnp.bfloat16).astype(jnp.float32).reshape(M, CH, 2, L)
        summed = jnp.einsum('mkcl,mla->mack', spec_half, legendre_wide, precision=HIGH)
        wave_grad = (summed * gauss_weights[None, :, None, None]).astype(jnp.bfloat16).astype(jnp.float32)
        tend_grad = jnp.einsum('mack,cmo->ako', wave_grad, table, precision=HIGH).astype(jnp.bfloat16).astype(jnp.float32)
        grid_wide = grid_one.astype(jnp.float32)
        pre_in = jnp.einsum('kh,ako->aho', w_in_wide, grid_wide, precision=HIGH) + bias_in[None, :, None]
        hidden_in = gelu_value(pre_in).astype(jnp.bfloat16).astype(jnp.float32)
        pre_mid = jnp.einsum('hg,aho->ago', w_mid_wide, hidden_in, precision=HIGH) + bias_mid[None, :, None]
        hidden_mid = gelu_value(pre_mid).astype(jnp.bfloat16).astype(jnp.float32)
        out_raw = jnp.einsum('ago,ako->gk', hidden_mid, tend_grad, precision=HIGH)
        back_mid = jnp.einsum('gk,ako->ago', w_out_wide, tend_grad, precision=HIGH)
        err_mid = (back_mid * gelu_slope(pre_mid)).astype(jnp.bfloat16).astype(jnp.float32)
        mid_raw = jnp.einsum('aho,ago->hg', hidden_in, err_mid, precision=HIGH)
        bmid_raw = lax.optimization_barrier(jnp.sum(err_mid, axis=(0, 2)))
        back_in = jnp.einsum('hg,ago->aho', w_mid_wide, err_mid, precision=HIGH)
        err_in = (back_in * gelu_slope(pre_in)).astype(jnp.bfloat16).astype(jnp.float32)
        in_raw = jnp.einsum('ako,aho->kh', grid_wide, err_in, precision=HIGH)
        bin_raw = lax.optimization_barrier(jnp.sum(err_in, axis=(0, 2)))
        state_grid = jnp.einsum('kh,aho->ako', w_in_wide, err_in, precision=HIGH).astype(jnp.bfloat16).astype(jnp.float32)
        wave_back = jnp.einsum('ako,cmo->mack', state_grid, table, precision=HIGH).astype(jnp.bfloat16).astype(jnp.float32)
        spectral = jnp.einsum('mack,mla->mkcl', wave_back, legendre_wide, precision=HIGH).reshape(M, CH, 2 * L)
        return (spec_grad + spectral, (in_raw, bin_raw, mid_raw, bmid_raw, out_raw))
    grad_state, raws = lax.map(one_state, (cotangent, grid_state))
    in_raw, bin_raw, mid_raw, bmid_raw, out_raw = [lax.optimization_barrier(jnp.sum(part, axis=0)) for part in raws]
    total = jnp.sum(in_raw * in_raw) + jnp.sum(bin_raw * bin_raw) + jnp.sum(mid_raw * mid_raw)
    total = total + jnp.sum(bmid_raw * bmid_raw) + jnp.sum(out_raw * out_raw)
    limit = math.sqrt(2 * CH * HID + HID * HID + 2 * HID)
    factor = jnp.minimum(jnp.float32(1.0), limit / jnp.sqrt(total + 1e-06))
    return (grad_state, factor * in_raw, factor * bin_raw, factor * mid_raw, factor * bmid_raw, factor * out_raw)
```

```python
import functools
import math

import jax
import jax.numpy as jnp
import numpy as np
from jax import lax
from jax.experimental import pallas as pl
from jax.experimental.pallas import tpu as pltpu
from jax.sharding import PartitionSpec as P

MESH = pl.DeviceIdType.MESH
F32 = jnp.float32
BF16 = jnp.bfloat16

Z, X, NB = 8, 4, 8
SP = Z * X
TRAJ, WAVE, LATS = 2, 6, 8
CHAN, HIDDEN, LONS, DEG = 128, 256, 512, 192
COEF = 2 * DEG
MC = 2 * WAVE * SP
SEG = 40
ROWS = 32 * SEG
LIMIT = math.sqrt(2 * CHAN * HIDDEN + HIDDEN * HIDDEN + 2 * HIDDEN)


def fourier_rows():
    waves = WAVE * SP
    phase = (np.arange(waves)[:, None] * np.arange(LONS)[None, :]) % LONS
    phase = phase * (2.0 * math.pi / LONS)
    table = np.stack([np.cos(phase), -np.sin(phase)], axis=1) / math.sqrt(waves)
    return table.reshape(MC, LONS).astype(np.float32)


def dot(a, b, ca, cb):
    return lax.dot_general(a, b, (((ca,), (cb,)), ((), ())), preferred_element_type=F32)


def column(row_ref):
    return jnp.broadcast_to(row_ref[...], (128, row_ref.shape[1])).T


def gelu_pair(v):
    square = v * v
    tanh_part = jnp.tanh(v * (0.7978845608 + 0.7978845608 * 0.044715 * square))
    up = 0.5 + 0.5 * tanh_part
    value = v * up
    bend = 0.7978845608 + 0.7978845608 * 0.134145 * square
    slope = up + 0.5 * v * (1.0 - tanh_part * tanh_part) * bend
    return value, slope


def kernel(
    cot_hbm, grid_hbm, leg_hbm, inv_hbm, gw_ref, w_in, b_in, w_mid, b_mid, w_out, tab,
    out_hbm, g_in, g_bin, g_mid, g_bmid, g_out,
    cot, grid, leg, inv, out, bd, send1, recv1, send2, recv2, wide,
    h_in, h_mid, s_in, s_mid, w_in_t, w_mid_t, col_g, col_in, col_mid,
    acc, acc_bin, acc_bmid, got_a, got_z, total,
    in_sem, out_sem, s1_sem, r1_sem, s2_sem, r2_sem, sa_sem, ra_sem, sz_sem, rz_sem, sc_sem, rc_sem,
):
    me = lax.axis_index("space")
    bat = lax.axis_index("batch")
    z, x = me // X, me % X
    gi = bat * X + x

    loads = [
        pltpu.make_async_copy(inv_hbm, inv, in_sem.at[0]),
        pltpu.make_async_copy(leg_hbm, leg, in_sem.at[1]),
        pltpu.make_async_copy(cot_hbm.at[0], cot.at[0], in_sem.at[2]),
        pltpu.make_async_copy(cot_hbm.at[1], cot.at[1], in_sem.at[3]),
        pltpu.make_async_copy(grid_hbm, grid, in_sem.at[4]),
    ]
    for load in loads:
        load.start()

    def space_peer(s):
        return lax.rem(me + s, SP)

    def group_peer(s):
        g = lax.rem(gi + s, 32)
        return g, (z * X + g % X, g // X)

    def depth_peer(s):
        return lax.rem(z + s, Z) * X + x

    barrier = pltpu.get_barrier_semaphore()

    def greet(s, carry):
        pl.semaphore_signal(barrier, inc=1, device_id=(space_peer(s), bat), device_id_type=MESH)
        pl.semaphore_signal(barrier, inc=1, device_id=group_peer(s)[1], device_id_type=MESH)
        return carry

    lax.fori_loop(1, 32, greet, 0)

    def copy1(b, s):
        peer = space_peer(s)
        return pltpu.make_async_remote_copy(
            src_ref=send1.at[b, peer], dst_ref=recv1.at[b, me],
            send_sem=s1_sem.at[b, s], recv_sem=r1_sem.at[b, s],
            device_id=(peer, bat), device_id_type=MESH,
        )

    def copy2(b, s):
        peer = space_peer(s)
        return pltpu.make_async_remote_copy(
            src_ref=send2.at[b, peer], dst_ref=recv2.at[b, me],
            send_sem=s2_sem.at[b, s], recv_sem=r2_sem.at[b, s],
            device_id=(peer, bat), device_id_type=MESH,
        )

    def copy_a(s):
        g, where = group_peer(s)
        return pltpu.make_async_remote_copy(
            src_ref=acc.at[pl.ds(pl.multiple_of(g * SEG, 8), SEG)], dst_ref=got_a.at[gi],
            send_sem=sa_sem.at[s], recv_sem=ra_sem.at[s], device_id=where, device_id_type=MESH,
        )

    def copy_z(s):
        return pltpu.make_async_remote_copy(
            src_ref=got_z.at[z], dst_ref=got_z.at[z],
            send_sem=sz_sem.at[s], recv_sem=rz_sem.at[s],
            device_id=(depth_peer(s), bat), device_id_type=MESH,
        )

    def copy_c(s):
        _, where = group_peer(s)
        mine = pl.ds(pl.multiple_of(gi * SEG, 8), SEG)
        return pltpu.make_async_remote_copy(
            src_ref=total.at[mine], dst_ref=total.at[mine],
            send_sem=sc_sem.at[s], recv_sem=rc_sem.at[s], device_id=where, device_id_type=MESH,
        )

    def each(first, last, act):
        def body(s, carry):
            act(s)
            return carry

        lax.fori_loop(first, last, body, 0)

    col_g[...] = column(gw_ref)
    loads[0].wait()
    loads[1].wait()
    lane = lax.broadcasted_iota(jnp.int32, (DEG, 2 * COEF), 1)
    row = lax.broadcasted_iota(jnp.int32, (DEG, 2 * COEF), 0)
    pick = jnp.where((lane == row) | (lane == row + COEF + DEG), 1.0, 0.0).astype(BF16)
    lane = lax.broadcasted_iota(jnp.int32, (32, CHAN), 1)
    row = lax.broadcasted_iota(jnp.int32, (32, CHAN), 0)
    repeat = jnp.where(lane % 32 == row, 1.0, 0.0).astype(BF16)
    lane = lax.broadcasted_iota(jnp.int32, (CHAN, CHAN), 1)
    row = lax.broadcasted_iota(jnp.int32, (CHAN, CHAN), 0)
    same = lane // 32 == row // 32

    def spectral_in(b, m):
        block = inv[m].reshape(CHAN, 32)
        high = block.astype(BF16)
        low = (block - high.astype(F32)).astype(BF16)
        high = jnp.where(same, dot(high, repeat, 1, 0), 0.0).T.astype(BF16)
        low = jnp.where(same, dot(low, repeat, 1, 0), 0.0).T.astype(BF16)
        value = cot[b, m]
        value_high = value.astype(BF16)
        value_low = (value - value_high.astype(F32)).astype(BF16)
        grad = dot(
            jnp.concatenate([high, low, high], axis=1),
            jnp.concatenate([value_high, value_high, value_low], axis=0),
            1, 0,
        )
        out[b, m] = grad
        if b == 0:
            turned = dot(leg[m], pick, 0, 0).reshape(SP, LATS, 2 * COEF)
            both = jnp.concatenate([turned[:, :, :COEF], turned[:, :, COEF:]], axis=1)
            bd[m] = both.reshape(2 * LATS * SP, COEF).astype(BF16)
        sums = dot(bd[m], grad.astype(BF16), 1, 1).reshape(SP, 2, LATS, CHAN)
        scaled = sums * col_g[...].reshape(SP, 1, LATS, CHAN)
        send1[b, :, m] = scaled.reshape(SP, 2 * LATS, CHAN).astype(BF16)

    for b in range(TRAJ):
        loads[2 + b].wait()
        each(0, WAVE, functools.partial(spectral_in, b))
        if b == 0:
            pl.semaphore_wait(barrier, 62)
        each(1, SP, lambda s: copy1(b, s).start())
        recv1[b, me] = send1[b, me]

    w_in_t[...] = w_in[...].T
    w_mid_t[...] = w_mid[...].T
    col_in[...] = column(b_in)
    col_mid[...] = column(b_mid)
    acc[...] = jnp.zeros_like(acc)
    acc_bin[...] = jnp.zeros_like(acc_bin)
    acc_bmid[...] = jnp.zeros_like(acc_bmid)
    loads[4].wait()

    def forward(i):
        b, a = i // LATS, i % LATS
        pre = dot(w_in_t[...], grid[b, a], 1, 0)
        value, slope = gelu_pair(pre + jnp.concatenate([col_in[...]] * 4, axis=1))
        hidden = value.astype(BF16)
        h_in[i] = hidden
        s_in[i] = slope
        pre = dot(w_mid_t[...], hidden, 1, 0)
        value, slope = gelu_pair(pre + jnp.concatenate([col_mid[...]] * 4, axis=1))
        h_mid[i] = value.astype(BF16)
        s_mid[i] = slope

    each(0, TRAJ * LATS, forward)

    def lane_sum(v):
        return v[:, :128] + v[:, 128:256] + v[:, 256:384] + v[:, 384:]

    def backward(b, a):
        i = b * LATS + a
        part = wide[pl.ds(a, MC, stride=LATS), :].astype(BF16)
        tend = dot(part, tab[...], 0, 0).astype(BF16)
        acc[768:1024] += dot(h_mid[i], tend, 1, 1)
        err_mid = (dot(w_out[...], tend, 1, 0) * s_mid[i]).astype(BF16)
        mid = dot(h_in[i], err_mid, 1, 1)
        acc[256:512] += mid[:, :128]
        acc[512:768] += mid[:, 128:]
        acc_bmid[...] += lane_sum(err_mid.astype(F32))
        err_in = (dot(w_mid[...], err_mid, 1, 0) * s_in[i]).astype(BF16)
        raw = dot(grid[b, a], err_in, 1, 1)
        acc[0:128] += raw[:, :128]
        acc[128:256] += raw[:, 128:]
        acc_bin[...] += lane_sum(err_in.astype(F32))
        state = dot(w_in[...], err_in, 1, 0).astype(BF16)
        wide[pl.ds(a, MC, stride=LATS), :] = dot(tab[...], state, 1, 1)

    per_peer = 2 * WAVE * LATS

    def unpack(b, peer):
        rows = pl.ds(pl.multiple_of(peer * per_peer, per_peer), per_peer)
        wide[rows, :] = recv1[b, peer].reshape(per_peer, CHAN).astype(F32)

    def pack(b, peer):
        rows = pl.ds(pl.multiple_of(peer * per_peer, per_peer), per_peer)
        send2[b, peer] = wide[rows, :].astype(BF16).reshape(WAVE, 2 * LATS, CHAN)

    for b in range(TRAJ):
        unpack(b, me)

        def arrive(s):
            copy1(b, s).wait_recv()
            unpack(b, lax.rem(me + SP - s, SP))

        each(1, SP, arrive)
        each(0, LATS, functools.partial(backward, b))
        if b == TRAJ - 1:
            bins = jnp.sum(acc_bin[...].T, axis=0, keepdims=True)
            bmids = jnp.sum(acc_bmid[...].T, axis=0, keepdims=True)
            acc[1024:1025] = bins[:, :128]
            acc[1025:1026] = bins[:, 128:]
            acc[1026:1027] = bmids[:, :128]
            acc[1027:1028] = bmids[:, 128:]
            each(1, 32, lambda s: copy_a(s).start())

        def depart(s):
            pack(b, space_peer(s))
            copy2(b, s).start()

        each(1, SP, depart)
        pack(b, me)
        recv2[b, me] = send2[b, me]

    def spectral_out(b, m):
        back = recv2[b, :, m].reshape(2 * LATS * SP, CHAN)
        out[b, m] += dot(back, bd[m], 0, 0)
        pltpu.make_async_copy(out.at[b, m], out_hbm.at[b, m], out_sem.at[b, m]).start()

    def finish(b):
        each(1, SP, lambda s: copy2(b, s).wait_recv())
        each(0, WAVE, functools.partial(spectral_out, b))

    mine = pl.ds(pl.multiple_of(gi * SEG, 8), SEG)
    got_a[gi] = acc[mine]
    each(1, 32, lambda s: copy_a(s).wait_recv())
    got_z[z] = lax.fori_loop(1, 32, lambda i, t: t + got_a[i], got_a[0])
    each(1, Z, lambda s: copy_z(s).start())
    finish(0)
    each(1, Z, lambda s: copy_z(s).wait_recv())
    total[mine] = lax.fori_loop(1, Z, lambda i, t: t + got_z[i], got_z[0])
    each(1, 32, lambda s: copy_c(s).start())
    finish(1)
    each(1, 32, lambda s: copy_c(s).wait_recv())
    squares = total[...] * total[...]
    factor = jnp.minimum(F32(1.0), LIMIT / jnp.sqrt(jnp.sum(squares, keepdims=True) + 1e-06))
    g_in[:, :128] = factor * total[0:128]
    g_in[:, 128:] = factor * total[128:256]
    g_mid[:, :128] = factor * total[256:512]
    g_mid[:, 128:] = factor * total[512:768]
    g_out[...] = factor * total[768:1024]
    g_bin[:, :128] = factor * total[1024:1025]
    g_bin[:, 128:] = factor * total[1025:1026]
    g_bmid[:, :128] = factor * total[1026:1027]
    g_bmid[:, 128:] = factor * total[1027:1028]

    for b in range(TRAJ):
        each(1, SP, lambda s: copy1(b, s).wait_send())
        each(1, SP, lambda s: copy2(b, s).wait_send())
        each(0, WAVE, lambda m: pltpu.make_async_copy(
            out.at[b, m], out_hbm.at[b, m], out_sem.at[b, m]).wait())
    each(1, 32, lambda s: copy_a(s).wait_send())
    each(1, Z, lambda s: copy_z(s).wait_send())
    each(1, 32, lambda s: copy_c(s).wait_send())


def shards(
    cotangent, grid_state, legendre, inverse, gauss_weights, w_in, bias_in, w_mid, bias_mid, w_out
):
    table = jnp.asarray(fourier_rows(), F32).astype(BF16)
    vmem = pl.BlockSpec(memory_space=pltpu.VMEM)
    hbm = pl.BlockSpec(memory_space=pl.ANY)
    cols = TRAJ * LATS
    message = (TRAJ, SP, WAVE, 2 * LATS, CHAN)
    dma = pltpu.SemaphoreType.DMA
    outs = pl.pallas_call(
        kernel,
        out_shape=(
            jax.ShapeDtypeStruct((TRAJ, WAVE, CHAN, COEF), F32),
            jax.ShapeDtypeStruct((CHAN, HIDDEN), F32),
            jax.ShapeDtypeStruct((1, HIDDEN), F32),
            jax.ShapeDtypeStruct((HIDDEN, HIDDEN), F32),
            jax.ShapeDtypeStruct((1, HIDDEN), F32),
            jax.ShapeDtypeStruct((HIDDEN, CHAN), F32),
        ),
        in_specs=[hbm] * 4 + [vmem] * 7,
        out_specs=[hbm] + [vmem] * 5,
        scratch_shapes=[
            pltpu.VMEM((TRAJ, WAVE, CHAN, COEF), F32),
            pltpu.VMEM((TRAJ, LATS, CHAN, LONS), BF16),
            pltpu.VMEM((WAVE, DEG, LATS * SP), BF16),
            pltpu.VMEM((WAVE, 4, 32, 32), F32),
            pltpu.VMEM((TRAJ, WAVE, CHAN, COEF), F32),
            pltpu.VMEM((WAVE, 2 * LATS * SP, COEF), BF16),
            pltpu.VMEM(message, BF16),
            pltpu.VMEM(message, BF16),
            pltpu.VMEM(message, BF16),
            pltpu.VMEM(message, BF16),
            pltpu.VMEM((MC * LATS, CHAN), F32),
            pltpu.VMEM((cols, HIDDEN, LONS), BF16),
            pltpu.VMEM((cols, HIDDEN, LONS), BF16),
            pltpu.VMEM((cols, HIDDEN, LONS), F32),
            pltpu.VMEM((cols, HIDDEN, LONS), F32),
            pltpu.VMEM((HIDDEN, CHAN), BF16),
            pltpu.VMEM((HIDDEN, HIDDEN), BF16),
            pltpu.VMEM((LATS * SP, 128), F32),
            pltpu.VMEM((HIDDEN, 128), F32),
            pltpu.VMEM((HIDDEN, 128), F32),
            pltpu.VMEM((ROWS, 128), F32),
            pltpu.VMEM((HIDDEN, 128), F32),
            pltpu.VMEM((HIDDEN, 128), F32),
            pltpu.VMEM((32, SEG, 128), F32),
            pltpu.VMEM((Z, SEG, 128), F32),
            pltpu.VMEM((ROWS, 128), F32),
            dma((5,)),
            dma((TRAJ, WAVE)),
            dma((TRAJ, SP)),
            dma((TRAJ, SP)),
            dma((TRAJ, SP)),
            dma((TRAJ, SP)),
            dma((32,)),
            dma((32,)),
            dma((Z,)),
            dma((Z,)),
            dma((32,)),
            dma((32,)),
        ],
        compiler_params=pltpu.CompilerParams(
            collective_id=0, has_side_effects=True, vmem_limit_bytes=60 * 1024 * 1024
        ),
    )(
        cotangent, grid_state, legendre, inverse, gauss_weights.reshape(1, -1),
        w_in, bias_in.reshape(1, -1), w_mid, bias_mid.reshape(1, -1), w_out, table,
    )
    state, g_in, g_bin, g_mid, g_bmid, g_out = outs
    return state, g_in, g_bin.reshape(-1), g_mid, g_bmid.reshape(-1), g_out


def solution(mesh):
    return jax.shard_map(
        shards,
        mesh=mesh,
        in_specs=(
            P("batch", "space", None, None),
            P("batch", "space", None, None),
            P("space", None, None),
            P("space", None, None, None),
            P(),
            P(),
            P(),
            P(),
            P(),
            P(),
        ),
        out_specs=(P("batch", "space", None, None), P(), P(), P(), P(), P()),
        check_vma=False,
    )
```

```python
import functools
import math

import jax
import jax.numpy as jnp
import numpy as np
from jax import lax
from jax.experimental import pallas as pl
from jax.experimental.pallas import tpu as pltpu
from jax.sharding import PartitionSpec as P

MESH = pl.DeviceIdType.MESH
F32 = jnp.float32
BF16 = jnp.bfloat16

Z, X, NB = 8, 4, 8
SP = Z * X
TRAJ, WAVE, LATS = 2, 6, 8
CHAN, HIDDEN, LONS, DEG = 128, 256, 512, 192
COEF = 2 * DEG
MC = 2 * WAVE * SP
SEG = 40
ROWS = 32 * SEG
HELD = 16
LIMIT = math.sqrt(2 * CHAN * HIDDEN + HIDDEN * HIDDEN + 2 * HIDDEN)


def fourier_rows():
    waves = WAVE * SP
    phase = (np.arange(waves)[:, None] * np.arange(LONS)[None, :]) % LONS
    phase = phase * (2.0 * math.pi / LONS)
    table = np.stack([np.cos(phase), -np.sin(phase)], axis=1) / math.sqrt(waves)
    return table.reshape(MC, LONS).astype(np.float32)


def dot(a, b, ca, cb):
    return lax.dot_general(a, b, (((ca,), (cb,)), ((), ())), preferred_element_type=F32)


def column(row_ref):
    return jnp.broadcast_to(row_ref[...], (128, row_ref.shape[1])).T


def gelu_pair(v):
    square = v * v
    tanh_part = jnp.tanh(v * (0.7978845608 + 0.7978845608 * 0.044715 * square))
    up = 0.5 + 0.5 * tanh_part
    value = v * up
    bend = 0.7978845608 + 0.7978845608 * 0.134145 * square
    slope = up + 0.5 * v * (1.0 - tanh_part * tanh_part) * bend
    return value, slope


def legendre_back(back, leg):
    wide = back.astype(F32)
    real = wide[:, :LATS].reshape(LATS * SP, CHAN)
    imag = wide[:, LATS:].reshape(LATS * SP, CHAN)
    sums = dot(jnp.concatenate([real, imag], axis=1).astype(BF16), leg, 0, 1)
    return jnp.concatenate([sums[:CHAN], sums[CHAN:]], axis=1)


def kernel(
    cot_hbm, grid_hbm, leg_hbm, inv_hbm, gw_hbm, w_in_hbm, b_in_hbm, w_mid_hbm, b_mid_hbm, w_out_hbm,
    tab_hbm, done_hbm, spec_hbm, back_hbm, total,
    cot, grid, leg, inv, gw, w_in, b_in, w_mid, b_mid, w_out, tab,
    spec, solve, send1, recv1, send2, recv2, wide,
    h_in, h_mid, s_in, s_mid, w_in_t, w_mid_t, col_g, col_in, col_mid,
    acc, acc_bin, acc_bmid, got_a, got_z,
    in_sem, out_sem, own_sem,
    s1_sem, r1_sem, s2_sem, r2_sem, sa_sem, ra_sem, sz_sem, rz_sem, sc_sem, rc_sem,
):
    me = lax.axis_index("space")
    bat = lax.axis_index("batch")
    z, x = me // X, me % X
    gi = bat * X + x

    loads = [
        pltpu.make_async_copy(source, target, in_sem.at[i])
        for i, (source, target) in enumerate([
            (inv_hbm, inv), (cot_hbm.at[0], cot.at[0]), (leg_hbm, leg), (gw_hbm, gw),
            (cot_hbm.at[1], cot.at[1]), (w_in_hbm, w_in), (b_in_hbm, b_in), (w_mid_hbm, w_mid),
            (b_mid_hbm, b_mid), (grid_hbm, grid), (w_out_hbm, w_out), (tab_hbm, tab),
        ])
    ]
    for load in loads:
        load.start()

    def shift(t):
        i, g = t % 8, t // 8
        return 4 + (1 - 2 * (i % 2)) * ((i + 1) // 2), g + i // 2

    def space_peer(t):
        dz, dx = shift(t)
        return (z + dz) % Z * X + (x + dx) % X

    def space_source(t):
        dz, dx = shift(t)
        return (z - dz + Z) % Z * X + (x - dx + 2 * X) % X

    def group_peer(s):
        g = (gi + s) % 32
        return g, (z * X + g % X, g // X)

    def depth_peer(s):
        return (z + s) % Z * X + x

    def each(first, last, act, unroll=1):
        def body(s, carry):
            act(s)
            return carry

        lax.fori_loop(first, last, body, 0, unroll=unroll)

    def peers(act, first=0, last=31):
        each(first, last, lambda t: act(t + (t + 17) // 32))

    barrier = pltpu.get_barrier_semaphore()

    def greet(t):
        pl.semaphore_signal(barrier, inc=1, device_id=(space_peer(t), bat), device_id_type=MESH)

    def greet_group(s):
        pl.semaphore_signal(barrier, inc=1, device_id=group_peer(s)[1], device_id_type=MESH)

    peers(greet)
    each(1, 32, greet_group)

    def copy1(b, s):
        peer = space_peer(s)
        return pltpu.make_async_remote_copy(
            src_ref=send1.at[b, peer], dst_ref=recv1.at[b, me],
            send_sem=s1_sem.at[b], recv_sem=r1_sem.at[b],
            device_id=(peer, bat), device_id_type=MESH,
        )

    def copy2(b, s):
        peer = space_peer(s)
        return pltpu.make_async_remote_copy(
            src_ref=send2.at[b, peer], dst_ref=recv2.at[me] if b == 0 else back_hbm.at[me],
            send_sem=s2_sem.at[b], recv_sem=r2_sem.at[b],
            device_id=(peer, bat), device_id_type=MESH,
        )

    def copy_a(s):
        g, where = group_peer(s)
        return pltpu.make_async_remote_copy(
            src_ref=acc.at[pl.ds(pl.multiple_of(g * SEG, 8), SEG)], dst_ref=got_a.at[gi],
            send_sem=sa_sem, recv_sem=ra_sem, device_id=where, device_id_type=MESH,
        )

    def copy_z(s):
        return pltpu.make_async_remote_copy(
            src_ref=got_z.at[z], dst_ref=got_z.at[z],
            send_sem=sz_sem, recv_sem=rz_sem,
            device_id=(depth_peer(s), bat), device_id_type=MESH,
        )

    def copy_c(s):
        _, where = group_peer(s)
        mine = pl.ds(pl.multiple_of(gi * SEG, 8), SEG)
        return pltpu.make_async_remote_copy(
            src_ref=total.at[mine], dst_ref=total.at[mine],
            send_sem=sc_sem, recv_sem=rc_sem, device_id=where, device_id_type=MESH,
        )

    def bulk(source, target, send_sem, recv_sem):
        return pltpu.make_async_remote_copy(
            src_ref=source, dst_ref=target, send_sem=send_sem, recv_sem=recv_sem,
            device_id=(space_peer(0), bat), device_id_type=MESH,
        )

    def all1(b):
        part = pl.ds(0, SP - 1)
        return bulk(send1.at[b, part], recv1.at[b, part], s1_sem.at[b], r1_sem.at[b])

    def all2(b):
        part = pl.ds(0, SP - 1)
        target = recv2.at[part] if b == 0 else back_hbm.at[part]
        return bulk(send2.at[b, part], target, s2_sem.at[b], r2_sem.at[b])

    def all_a():
        return bulk(acc.at[pl.ds(0, 31 * SEG)], got_a.at[pl.ds(0, 31)], sa_sem, ra_sem)

    def all_z():
        return bulk(got_z.at[pl.ds(0, Z - 1)], got_z.at[pl.ds(0, Z - 1)], sz_sem, rz_sem)

    def all_c():
        part = pl.ds(0, 31 * SEG)
        return bulk(total.at[part], total.at[part], sc_sem, rc_sem)

    lane = lax.broadcasted_iota(jnp.int32, (32, CHAN), 1)
    row = lax.broadcasted_iota(jnp.int32, (32, CHAN), 0)
    repeat = jnp.where(lane % 32 == row, 1.0, 0.0).astype(BF16)
    lane = lax.broadcasted_iota(jnp.int32, (CHAN, CHAN), 1)
    row = lax.broadcasted_iota(jnp.int32, (CHAN, CHAN), 0)
    same = lane // 32 == row // 32

    def spectral_in(b, m):
        if b == 0:
            block = inv[m].reshape(CHAN, 32)
            high = block.astype(BF16)
            low = (block - high.astype(F32)).astype(BF16)
            high = jnp.where(same, dot(high, repeat, 1, 0), 0.0).T.astype(BF16)
            low = jnp.where(same, dot(low, repeat, 1, 0), 0.0).T.astype(BF16)
            solve[m] = jnp.concatenate([high, low, high], axis=1)
        value = cot[b, m]
        value_high = value.astype(BF16)
        value_low = (value - value_high.astype(F32)).astype(BF16)
        grad = dot(
            solve[m], jnp.concatenate([value_high, value_high, value_low], axis=0), 1, 0
        )
        spec[b, m] = grad
        half = grad.astype(BF16)
        half = jnp.concatenate([half[:, :DEG], half[:, DEG:]], axis=0)
        sums = dot(leg[m], half, 0, 1)
        scaled = (sums * jnp.concatenate([col_g[...]] * 2, axis=1)).reshape(SP, LATS, 2 * CHAN)
        scaled = jnp.concatenate([scaled[:, :, :CHAN], scaled[:, :, CHAN:]], axis=1)
        send1[b, :, m] = scaled.astype(BF16)
        if b == 1:
            pltpu.make_async_copy(spec.at[1, m], spec_hbm.at[m], out_sem.at[1, m]).start()

    for load in loads[:4]:
        load.wait()
    col_g[...] = column(gw)
    for b in range(TRAJ):
        if b == 1:
            loads[4].wait()
        for m in range(WAVE):
            spectral_in(b, m)
        if b == 0:
            pl.semaphore_wait(barrier, 62)
        peers(lambda t: copy1(b, t).start())
        recv1[b, me] = send1[b, me]

    for load in loads[5:]:
        load.wait()
    w_in_t[...] = w_in[...].T
    w_mid_t[...] = w_mid[...].T
    col_in[...] = column(b_in)
    col_mid[...] = column(b_mid)
    acc[...] = jnp.zeros_like(acc)
    acc_bin[...] = jnp.zeros_like(acc_bin)
    acc_bmid[...] = jnp.zeros_like(acc_bmid)
    def forward(i):
        b, a = i // LATS, i % LATS
        pre = dot(w_in_t[...], grid[b, a], 1, 0)
        value, slope = gelu_pair(pre + jnp.concatenate([col_in[...]] * 4, axis=1))
        hidden = value.astype(BF16)
        h_in[i] = hidden
        s_in[i] = slope
        pre = dot(w_mid_t[...], hidden, 1, 0)
        value, slope = gelu_pair(pre + jnp.concatenate([col_mid[...]] * 4, axis=1))
        h_mid[i] = value.astype(BF16)
        s_mid[i] = slope

    each(0, TRAJ * LATS, forward)

    def lane_sum(v):
        return v[:, :128] + v[:, 128:256] + v[:, 256:384] + v[:, 384:]

    def backward(b, a):
        i = b * LATS + a
        part = wide[pl.ds(a, MC, stride=LATS), :].astype(BF16)
        tend = dot(part, tab[...], 0, 0).astype(BF16)
        acc[768:1024] += dot(h_mid[i], tend, 1, 1)
        err_mid = (dot(w_out[...], tend, 1, 0) * s_mid[i]).astype(BF16)
        mid = dot(h_in[i], err_mid, 1, 1)
        acc[256:512] += mid[:, :128]
        acc[512:768] += mid[:, 128:]
        acc_bmid[...] += lane_sum(err_mid.astype(F32))
        err_in = (dot(w_mid[...], err_mid, 1, 0) * s_in[i]).astype(BF16)
        raw = dot(grid[b, a], err_in, 1, 1)
        acc[0:128] += raw[:, :128]
        acc[128:256] += raw[:, 128:]
        acc_bin[...] += lane_sum(err_in.astype(F32))
        state = dot(w_in[...], err_in, 1, 0).astype(BF16)
        wide[pl.ds(a, MC, stride=LATS), :] = dot(tab[...], state, 1, 1)

    per_peer = 2 * WAVE * LATS

    def unpack(b, peer):
        rows = pl.ds(pl.multiple_of(peer * per_peer, per_peer), per_peer)
        wide[rows, :] = recv1[b, peer].reshape(per_peer, CHAN).astype(F32)

    def pack(b, peer):
        rows = pl.ds(pl.multiple_of(peer * per_peer, per_peer), per_peer)
        send2[b, peer] = wide[rows, :].astype(BF16).reshape(WAVE, 2 * LATS, CHAN)

    for b in range(TRAJ):
        all1(b).wait_recv()
        each(0, SP, functools.partial(unpack, b), 4)
        each(0, LATS, functools.partial(backward, b), 2)

        def depart(t):
            pack(b, space_peer(t))
            copy2(b, t).start()

        if b == 0:
            peers(depart)
            pack(b, me)
            recv2[me] = send2[b, me]

    bins = jnp.sum(acc_bin[...].T, axis=0, keepdims=True)
    bmids = jnp.sum(acc_bmid[...].T, axis=0, keepdims=True)
    acc[1024:1025] = bins[:, :128]
    acc[1025:1026] = bins[:, 128:]
    acc[1026:1027] = bmids[:, :128]
    acc[1027:1028] = bmids[:, 128:]
    each(1, 32, lambda s: copy_a(s).start())
    peers(depart, 0, HELD)
    pack(1, me)
    own = pltpu.make_async_copy(send2.at[1, me], back_hbm.at[me], own_sem)
    own.start()
    mine = pl.ds(pl.multiple_of(gi * SEG, 8), SEG)
    got_a[gi] = acc[mine]
    all_a().wait_recv()
    got_z[z] = lax.fori_loop(1, 32, lambda i, t: t + got_a[i], got_a[0])
    each(1, Z, lambda s: copy_z(s).start())
    peers(depart, HELD, 31)

    def finish(m):
        spec[0, m] += legendre_back(recv2[:, m], leg[m])
        pltpu.make_async_copy(spec.at[0, m], done_hbm.at[m], out_sem.at[0, m]).start()

    all2(0).wait_recv()
    for m in range(WAVE):
        finish(m)
    all_z().wait_recv()
    total[mine] = lax.fori_loop(1, Z, lambda i, t: t + got_z[i], got_z[0])
    each(1, 32, lambda s: copy_c(s).start())
    own.wait()
    for b in range(TRAJ):
        all1(b).wait_send()
        all2(b).wait_send()
    for m in range(WAVE):
        pltpu.make_async_copy(spec.at[0, m], done_hbm.at[m], out_sem.at[0, m]).wait()
        pltpu.make_async_copy(spec.at[1, m], spec_hbm.at[m], out_sem.at[1, m]).wait()
    all_a().wait_send()
    all_z().wait_send()
    all_c().wait_recv()
    all_c().wait_send()
    all2(1).wait_recv()


def last_kernel(
    done_hbm, spec_hbm, back_hbm, leg_hbm, total_hbm,
    out_hbm, g_in, g_bin, g_mid, g_bmid, g_out,
    held, spec, back, leg, total, sem, out_sem, done_sem, total_sem,
):
    done = pltpu.make_async_copy(done_hbm, held, done_sem.at[0])
    store = pltpu.make_async_copy(held, out_hbm.at[0], done_sem.at[1])
    loads = [
        [
            pltpu.make_async_copy(back_hbm.at[:, m], back.at[:, m], sem.at[m, 0]),
            pltpu.make_async_copy(leg_hbm.at[m], leg.at[m], sem.at[m, 1]),
            pltpu.make_async_copy(spec_hbm.at[m], spec.at[m], sem.at[m, 2]),
        ]
        for m in range(WAVE)
    ]
    sums = pltpu.make_async_copy(total_hbm, total, total_sem)
    for load in loads[0]:
        load.start()
    done.start()
    for load in sum(loads[1:], []):
        load.start()
    sums.start()
    stores = [store]
    for m in range(WAVE):
        for load in loads[m]:
            load.wait()
        spec[m] += legendre_back(back[:, m], leg[m])
        stores.append(pltpu.make_async_copy(spec.at[m], out_hbm.at[1, m], out_sem.at[m]))
        stores[-1].start()
        if m == 0:
            done.wait()
            store.start()
    sums.wait()
    squares = total[...] * total[...]
    factor = jnp.minimum(F32(1.0), LIMIT / jnp.sqrt(jnp.sum(squares, keepdims=True) + 1e-06))
    g_in[:, :128] = factor * total[0:128]
    g_in[:, 128:] = factor * total[128:256]
    g_mid[:, :128] = factor * total[256:512]
    g_mid[:, 128:] = factor * total[512:768]
    g_out[...] = factor * total[768:1024]
    g_bin[:, :128] = factor * total[1024:1025]
    g_bin[:, 128:] = factor * total[1025:1026]
    g_bmid[:, :128] = factor * total[1026:1027]
    g_bmid[:, 128:] = factor * total[1027:1028]
    for store in stores:
        store.wait()


def shards(
    cotangent, grid_state, legendre, inverse, gauss_weights, w_in, bias_in, w_mid, bias_mid, w_out
):
    table = jnp.asarray(fourier_rows(), F32).astype(BF16)
    vmem = pl.BlockSpec(memory_space=pltpu.VMEM)
    hbm = pl.BlockSpec(memory_space=pl.ANY)
    cols = TRAJ * LATS
    message = (TRAJ, SP, WAVE, 2 * LATS, CHAN)
    dma = pltpu.SemaphoreType.DMA
    state_half = jax.ShapeDtypeStruct((WAVE, CHAN, COEF), F32)
    done, spec, back, total = pl.pallas_call(
        kernel,
        name="exchange",
        out_shape=(
            state_half,
            state_half,
            jax.ShapeDtypeStruct(message[1:], BF16),
            jax.ShapeDtypeStruct((ROWS, 128), F32),
        ),
        in_specs=[hbm] * 11,
        out_specs=[hbm] * 3 + [vmem],
        scratch_shapes=[
            pltpu.VMEM((TRAJ, WAVE, CHAN, COEF), F32),
            pltpu.VMEM((TRAJ, LATS, CHAN, LONS), BF16),
            pltpu.VMEM((WAVE, DEG, LATS * SP), BF16),
            pltpu.VMEM((WAVE, 4, 32, 32), F32),
            pltpu.VMEM((1, LATS * SP), F32),
            pltpu.VMEM((CHAN, HIDDEN), BF16),
            pltpu.VMEM((1, HIDDEN), F32),
            pltpu.VMEM((HIDDEN, HIDDEN), BF16),
            pltpu.VMEM((1, HIDDEN), F32),
            pltpu.VMEM((HIDDEN, CHAN), BF16),
            pltpu.VMEM((MC, LONS), BF16),
            pltpu.VMEM((TRAJ, WAVE, CHAN, COEF), F32),
            pltpu.VMEM((WAVE, CHAN, 3 * CHAN), BF16),
            pltpu.VMEM(message, BF16),
            pltpu.VMEM(message, BF16),
            pltpu.VMEM(message, BF16),
            pltpu.VMEM(message[1:], BF16),
            pltpu.VMEM((MC * LATS, CHAN), F32),
            pltpu.VMEM((cols, HIDDEN, LONS), BF16),
            pltpu.VMEM((cols, HIDDEN, LONS), BF16),
            pltpu.VMEM((cols, HIDDEN, LONS), F32),
            pltpu.VMEM((cols, HIDDEN, LONS), F32),
            pltpu.VMEM((HIDDEN, CHAN), BF16),
            pltpu.VMEM((HIDDEN, HIDDEN), BF16),
            pltpu.VMEM((LATS * SP, 128), F32),
            pltpu.VMEM((HIDDEN, 128), F32),
            pltpu.VMEM((HIDDEN, 128), F32),
            pltpu.VMEM((ROWS, 128), F32),
            pltpu.VMEM((HIDDEN, 128), F32),
            pltpu.VMEM((HIDDEN, 128), F32),
            pltpu.VMEM((32, SEG, 128), F32),
            pltpu.VMEM((Z, SEG, 128), F32),
            dma((12,)),
            dma((TRAJ, WAVE)),
            dma,
            dma((TRAJ,)),
            dma((TRAJ,)),
            dma((TRAJ,)),
            dma((TRAJ,)),
            dma,
            dma,
            dma,
            dma,
            dma,
            dma,
        ],
        compiler_params=pltpu.CompilerParams(
            collective_id=0, has_side_effects=True, vmem_limit_bytes=60 * 1024 * 1024
        ),
    )(
        cotangent, grid_state, legendre, inverse, gauss_weights.reshape(1, -1),
        w_in, bias_in.reshape(1, -1), w_mid, bias_mid.reshape(1, -1), w_out, table,
    )
    state, g_in, g_bin, g_mid, g_bmid, g_out = pl.pallas_call(
        last_kernel,
        name="finish",
        out_shape=(
            jax.ShapeDtypeStruct((TRAJ, WAVE, CHAN, COEF), F32),
            jax.ShapeDtypeStruct((CHAN, HIDDEN), F32),
            jax.ShapeDtypeStruct((1, HIDDEN), F32),
            jax.ShapeDtypeStruct((HIDDEN, HIDDEN), F32),
            jax.ShapeDtypeStruct((1, HIDDEN), F32),
            jax.ShapeDtypeStruct((HIDDEN, CHAN), F32),
        ),
        in_specs=[hbm] * 5,
        out_specs=[hbm] + [vmem] * 5,
        scratch_shapes=[
            pltpu.VMEM((WAVE, CHAN, COEF), F32),
            pltpu.VMEM((WAVE, CHAN, COEF), F32),
            pltpu.VMEM(message[1:], BF16),
            pltpu.VMEM((WAVE, DEG, LATS * SP), BF16),
            pltpu.VMEM((ROWS, 128), F32),
            dma((WAVE, 3)),
            dma((WAVE,)),
            dma((2,)),
            dma,
        ],
        compiler_params=pltpu.CompilerParams(vmem_limit_bytes=60 * 1024 * 1024),
    )(done, spec, back, legendre, total)
    return state, g_in, g_bin.reshape(-1), g_mid, g_bmid.reshape(-1), g_out


def solution(mesh):
    return jax.shard_map(
        shards,
        mesh=mesh,
        in_specs=(
            P("batch", "space", None, None),
            P("batch", "space", None, None),
            P("space", None, None),
            P("space", None, None, None),
            P(),
            P(),
            P(),
            P(),
            P(),
            P(),
        ),
        out_specs=(P("batch", "space", None, None), P(), P(), P(), P(), P()),
        check_vma=False,
    )
```

```python
import functools
import math

import jax
import jax.numpy as jnp
import numpy as np
from jax import lax
from jax.experimental import pallas as pl
from jax.experimental.pallas import tpu as pltpu
from jax.sharding import PartitionSpec as P

MESH = pl.DeviceIdType.MESH
F32 = jnp.float32
BF16 = jnp.bfloat16

Z, X, NB = 8, 4, 8
SP = Z * X
TRAJ, WAVE, LATS = 2, 6, 8
HALF = LATS // 2
CHAN, HIDDEN, LONS, DEG = 128, 256, 512, 192
COEF = 2 * DEG
MC = 2 * WAVE * SP
SEG = 48
ROWS = 32 * SEG
HELD = 16
LIMIT = math.sqrt(2 * CHAN * HIDDEN + HIDDEN * HIDDEN + 2 * HIDDEN)


def fourier_rows():
    waves = WAVE * SP
    phase = (np.arange(waves)[:, None] * np.arange(LONS)[None, :]) % LONS
    phase = phase * (2.0 * math.pi / LONS)
    table = np.stack([np.cos(phase), -np.sin(phase)], axis=1) / math.sqrt(waves)
    return table.reshape(MC, LONS).astype(np.float32)


def dot(a, b, ca, cb):
    return lax.dot_general(a, b, (((ca,), (cb,)), ((), ())), preferred_element_type=F32)


def column(row_ref):
    return jnp.broadcast_to(row_ref[...], (128, row_ref.shape[1])).T


def gelu_pair(v):
    square = v * v
    tanh_part = jnp.tanh(v * (0.7978845608 + 0.7978845608 * 0.044715 * square))
    up = 0.5 + 0.5 * tanh_part
    value = v * up
    bend = 0.7978845608 + 0.7978845608 * 0.134145 * square
    slope = up + 0.5 * v * (1.0 - tanh_part * tanh_part) * bend
    return value, slope


def swap_halves(a, b):
    first = lax.broadcasted_iota(jnp.int32, a.shape, 1) < 4
    return jnp.where(first, a, pltpu.roll(b, 4, 1)), jnp.where(first, pltpu.roll(a, 4, 1), b)


def legendre_back(low, high, leg):
    real, imag = swap_halves(low, high)
    both = jnp.concatenate([real, imag], axis=2).reshape(LATS * SP, 2 * CHAN)
    sums = dot(both.astype(BF16), leg, 0, 1)
    return jnp.concatenate([sums[:CHAN], sums[CHAN:]], axis=1)


def sum_of(ref, count):
    first = ref[0].astype(F32)
    whole = lax.fori_loop(1, count, lambda i, t: t + ref[i].astype(F32), first)
    return whole.astype(BF16)


def kernel(
    cot_hbm, grid_hbm, leg_hbm, inv_hbm, gw_hbm, w_in_hbm, b_in_hbm, w_mid_hbm, b_mid_hbm, w_out_hbm,
    tab_hbm, done_hbm, spec_hbm, back_hbm, total,
    cot, grid, leg, inv, gw, w_in, b_in, w_mid, b_mid, w_out, tab,
    spec, solve, send1, recv1, send2, recv2, wide,
    h_in, h_mid, s_in, s_mid, w_in_t, w_mid_t, col_g, col_in, col_mid,
    acc, acc_bin, acc_bmid, parts, got_a, got_z,
    in_sem, out_sem, own_sem,
    s1_sem, r1_sem, s2_sem, r2_sem, sa_sem, ra_sem, sz_sem, rz_sem, sc_sem, rc_sem,
):
    me = lax.axis_index("space")
    bat = lax.axis_index("batch")
    z, x = me // X, me % X
    gi = bat * X + x

    loads = [
        pltpu.make_async_copy(source, target, in_sem.at[i])
        for i, (source, target) in enumerate([
            (inv_hbm, inv), (cot_hbm.at[0], cot.at[0]), (leg_hbm, leg), (gw_hbm, gw),
            (cot_hbm.at[1], cot.at[1]), (w_in_hbm, w_in), (b_in_hbm, b_in), (w_mid_hbm, w_mid),
            (b_mid_hbm, b_mid), (grid_hbm, grid), (w_out_hbm, w_out), (tab_hbm, tab),
        ])
    ]
    for load in loads:
        load.start()

    def shift(t):
        i, g = t % 8, t // 8
        return 4 + (1 - 2 * (i % 2)) * ((i + 1) // 2), g + i // 2

    def space_peer(t):
        dz, dx = shift(t)
        return (z + dz) % Z * X + (x + dx) % X

    def group_peer(s):
        g = (gi + s) % 32
        return g, (z * X + g % X, g // X)

    def depth_peer(s):
        return (z + s) % Z * X + x

    def each(first, last, act, unroll=1):
        def body(s, carry):
            act(s)
            return carry

        lax.fori_loop(first, last, body, 0, unroll=unroll)

    def peers(act, first=0, last=31):
        each(first, last, lambda t: act(t + (t + 17) // 32))

    barrier = pltpu.get_barrier_semaphore()

    def greet(t):
        pl.semaphore_signal(barrier, inc=1, device_id=(space_peer(t), bat), device_id_type=MESH)

    def greet_group(s):
        pl.semaphore_signal(barrier, inc=1, device_id=group_peer(s)[1], device_id_type=MESH)

    peers(greet)
    each(1, 32, greet_group)

    def copy1(q, s):
        peer = space_peer(s)
        return pltpu.make_async_remote_copy(
            src_ref=send1.at[q, peer], dst_ref=recv1.at[q, me],
            send_sem=s1_sem.at[q], recv_sem=r1_sem.at[q],
            device_id=(peer, bat), device_id_type=MESH,
        )

    def copy2(q, s):
        peer = space_peer(s)
        return pltpu.make_async_remote_copy(
            src_ref=send2.at[q, peer],
            dst_ref=recv2.at[q, me] if q < 2 else back_hbm.at[q - 2, me],
            send_sem=s2_sem.at[q], recv_sem=r2_sem.at[q],
            device_id=(peer, bat), device_id_type=MESH,
        )

    def copy_a(s):
        g, where = group_peer(s)
        return pltpu.make_async_remote_copy(
            src_ref=parts.at[pl.ds(pl.multiple_of(g * SEG, SEG), SEG)], dst_ref=got_a.at[gi],
            send_sem=sa_sem, recv_sem=ra_sem, device_id=where, device_id_type=MESH,
        )

    def copy_z(s):
        return pltpu.make_async_remote_copy(
            src_ref=got_z.at[z], dst_ref=got_z.at[z],
            send_sem=sz_sem, recv_sem=rz_sem,
            device_id=(depth_peer(s), bat), device_id_type=MESH,
        )

    def copy_c(s):
        _, where = group_peer(s)
        mine = pl.ds(pl.multiple_of(gi * SEG, SEG), SEG)
        return pltpu.make_async_remote_copy(
            src_ref=total.at[mine], dst_ref=total.at[mine],
            send_sem=sc_sem, recv_sem=rc_sem, device_id=where, device_id_type=MESH,
        )

    def bulk(source, target, send_sem, recv_sem):
        return pltpu.make_async_remote_copy(
            src_ref=source, dst_ref=target, send_sem=send_sem, recv_sem=recv_sem,
            device_id=(space_peer(0), bat), device_id_type=MESH,
        )

    def all1(q):
        part = pl.ds(0, SP - 1)
        return bulk(send1.at[q, part], recv1.at[q, part], s1_sem.at[q], r1_sem.at[q])

    def all2(q):
        part = pl.ds(0, SP - 1)
        target = recv2.at[q, part] if q < 2 else back_hbm.at[q - 2, part]
        return bulk(send2.at[q, part], target, s2_sem.at[q], r2_sem.at[q])

    def all_a():
        return bulk(parts.at[pl.ds(0, 31 * SEG)], got_a.at[pl.ds(0, 31)], sa_sem, ra_sem)

    def all_z():
        return bulk(got_z.at[pl.ds(0, Z - 1)], got_z.at[pl.ds(0, Z - 1)], sz_sem, rz_sem)

    def all_c():
        part = pl.ds(0, 31 * SEG)
        return bulk(total.at[part], total.at[part], sc_sem, rc_sem)

    lane = lax.broadcasted_iota(jnp.int32, (32, CHAN), 1)
    row = lax.broadcasted_iota(jnp.int32, (32, CHAN), 0)
    repeat = jnp.where(lane % 32 == row, 1.0, 0.0).astype(BF16)
    lane = lax.broadcasted_iota(jnp.int32, (CHAN, CHAN), 1)
    row = lax.broadcasted_iota(jnp.int32, (CHAN, CHAN), 0)
    same = lane // 32 == row // 32

    def spectral_in(b, m):
        if b == 0:
            block = inv[m].reshape(CHAN, 32)
            high = block.astype(BF16)
            low = (block - high.astype(F32)).astype(BF16)
            high = jnp.where(same, dot(high, repeat, 1, 0), 0.0).T.astype(BF16)
            low = jnp.where(same, dot(low, repeat, 1, 0), 0.0).T.astype(BF16)
            solve[m] = jnp.concatenate([high, low, high], axis=1)
        value = cot[b, m]
        value_high = value.astype(BF16)
        value_low = (value - value_high.astype(F32)).astype(BF16)
        grad = dot(
            solve[m], jnp.concatenate([value_high, value_high, value_low], axis=0), 1, 0
        )
        spec[b, m] = grad
        half = grad.astype(BF16)
        half = jnp.concatenate([half[:, :DEG], half[:, DEG:]], axis=0)
        sums = dot(leg[m], half, 0, 1)
        scaled = (sums * jnp.concatenate([col_g[...]] * 2, axis=1)).reshape(SP, LATS, 2 * CHAN)
        if b == 1:
            pltpu.make_async_copy(spec.at[1, m], spec_hbm.at[m], out_sem.at[1, m]).start()
        return swap_halves(scaled[:, :, :CHAN], scaled[:, :, CHAN:])

    for load in loads[:4]:
        load.wait()
    col_g[...] = column(gw)
    for b in range(TRAJ):
        if b == 1:
            loads[4].wait()
        for m in range(0, WAVE, 2):
            for h, pair in enumerate(zip(spectral_in(b, m), spectral_in(b, m + 1), strict=True)):
                send1[2 * b + h, :, 8 * m : 8 * m + 16] = jnp.concatenate(pair, axis=1).astype(BF16)
        if b == 0:
            pl.semaphore_wait(barrier, 62)
        if b == 0:
            peers(lambda t: copy1(0, t).start())
            peers(lambda t: copy1(1, t).start())
        for q in (2 * b, 2 * b + 1):
            recv1[q, me] = send1[q, me]

    for load in loads[5:]:
        load.wait()
    w_in_t[...] = w_in[...].T
    w_mid_t[...] = w_mid[...].T
    col_in[...] = column(b_in)
    col_mid[...] = column(b_mid)
    acc[...] = jnp.zeros_like(acc)
    acc_bin[...] = jnp.zeros_like(acc_bin)
    acc_bmid[...] = jnp.zeros_like(acc_bmid)
    def forward(i):
        b, a = i // LATS, i % LATS
        first = 4 * (i % 8)

        @pl.when(i < 8)
        def _():
            peers(lambda t: copy1(2, t).start(), first, jnp.minimum(first + 4, 31))

        @pl.when(i >= 8)
        def _():
            peers(lambda t: copy1(3, t).start(), first, jnp.minimum(first + 4, 31))

        pre = dot(w_in_t[...], grid[b, a], 1, 0)
        value, slope = gelu_pair(pre + jnp.concatenate([col_in[...]] * 4, axis=1))
        hidden = value.astype(BF16)
        h_in[i] = hidden
        s_in[i] = slope
        pre = dot(w_mid_t[...], hidden, 1, 0)
        value, slope = gelu_pair(pre + jnp.concatenate([col_mid[...]] * 4, axis=1))
        h_mid[i] = value.astype(BF16)
        s_mid[i] = slope

    each(0, TRAJ * LATS, forward)

    def lane_sum(v):
        return v[:, :128] + v[:, 128:256] + v[:, 256:384] + v[:, 384:]

    def backward(q, a):
        i = q * HALF + a
        rows = pl.ds(a, MC, stride=HALF)
        part = wide[rows, :].astype(BF16)
        tend = dot(part, tab[...], 0, 0).astype(BF16)
        acc[768:1024] += dot(h_mid[i], tend, 1, 1)
        err_mid = (dot(w_out[...], tend, 1, 0) * s_mid[i]).astype(BF16)
        mid = dot(h_in[i], err_mid, 1, 1)
        acc[256:512] += mid[:, :128]
        acc[512:768] += mid[:, 128:]
        acc_bmid[...] += lane_sum(err_mid.astype(F32))
        err_in = (dot(w_mid[...], err_mid, 1, 0) * s_in[i]).astype(BF16)
        raw = dot(grid[q // 2, q % 2 * HALF + a], err_in, 1, 1)
        acc[0:128] += raw[:, :128]
        acc[128:256] += raw[:, 128:]
        acc_bin[...] += lane_sum(err_in.astype(F32))
        state = dot(w_in[...], err_in, 1, 0).astype(BF16)
        wide[rows, :] = dot(tab[...], state, 1, 1)

    per_peer = 2 * WAVE * HALF

    def unpack(q, peer):
        rows = pl.ds(pl.multiple_of(peer * per_peer, per_peer), per_peer)
        wide[rows, :] = recv1[q, peer].astype(F32)

    def pack(q, peer):
        rows = pl.ds(pl.multiple_of(peer * per_peer, per_peer), per_peer)
        send2[q, peer] = wide[rows, :].astype(BF16)

    def depart(q, t):
        pack(q, space_peer(t))
        copy2(q, t).start()

    for q in range(2 * TRAJ):
        all1(q).wait_recv()
        each(0, SP, functools.partial(unpack, q), 4)
        each(0, HALF, functools.partial(backward, q), HALF)
        if q < 3:
            peers(functools.partial(depart, q))
            pack(q, me)
            if q < 2:
                recv2[q, me] = send2[q, me]

    bins = jnp.sum(acc_bin[...].T, axis=0, keepdims=True)
    bmids = jnp.sum(acc_bmid[...].T, axis=0, keepdims=True)
    acc[1024:1025] = bins[:, :128]
    acc[1025:1026] = bins[:, 128:]
    acc[1026:1027] = bmids[:, :128]
    acc[1027:1028] = bmids[:, 128:]
    parts[...] = acc[...].astype(BF16)
    each(1, 32, lambda s: copy_a(s).start())
    peers(functools.partial(depart, 3), 0, HELD)
    pack(3, me)
    own = pltpu.make_async_copy(send2.at[pl.ds(2, 2), me], back_hbm.at[:, me], own_sem)
    own.start()
    mine = pl.ds(pl.multiple_of(gi * SEG, SEG), SEG)
    got_a[gi] = parts[mine]
    all_a().wait_recv()
    got_z[z] = sum_of(got_a, 32)
    each(1, Z, lambda s: copy_z(s).start())
    peers(functools.partial(depart, 3), HELD, 31)

    all2(0).wait_recv()
    all2(1).wait_recv()
    for m in range(WAVE):
        if m % 2 == 0:
            back = recv2[:, :, 8 * m : 8 * m + 16].astype(F32)
        rows = slice(m % 2 * 8, m % 2 * 8 + 8)
        spec[0, m] += legendre_back(back[0, :, rows], back[1, :, rows], leg[m])
        pltpu.make_async_copy(spec.at[0, m], done_hbm.at[m], out_sem.at[0, m]).start()
    all_z().wait_recv()
    total[mine] = sum_of(got_z, Z)
    each(1, 32, lambda s: copy_c(s).start())
    own.wait()
    for q in range(2 * TRAJ):
        all1(q).wait_send()
        all2(q).wait_send()
    for m in range(WAVE):
        pltpu.make_async_copy(spec.at[0, m], done_hbm.at[m], out_sem.at[0, m]).wait()
        pltpu.make_async_copy(spec.at[1, m], spec_hbm.at[m], out_sem.at[1, m]).wait()
    all_a().wait_send()
    all_z().wait_send()
    all_c().wait_recv()
    all_c().wait_send()
    all2(2).wait_recv()
    all2(3).wait_recv()


def last_kernel(
    done_hbm, spec_hbm, back_hbm, leg_hbm, total_hbm,
    out_hbm, g_in, g_bin, g_mid, g_bmid, g_out,
    held, spec, back, leg, total, sem, pair_sem, out_sem, done_sem, total_sem,
):
    done = pltpu.make_async_copy(done_hbm, held, done_sem.at[0])
    store = pltpu.make_async_copy(held, out_hbm.at[0], done_sem.at[1])
    pairs = [
        pltpu.make_async_copy(back_hbm.at[:, :, rows], back.at[:, :, rows], pair_sem.at[p])
        for p, rows in enumerate([pl.ds(0, 16), pl.ds(16, 16), pl.ds(32, 16)])
    ]
    loads = [
        ([pairs[m // 2]] if m % 2 == 0 else []) + [
            pltpu.make_async_copy(leg_hbm.at[m], leg.at[m], sem.at[m, 0]),
            pltpu.make_async_copy(spec_hbm.at[m], spec.at[m], sem.at[m, 1]),
        ]
        for m in range(WAVE)
    ]
    sums = pltpu.make_async_copy(total_hbm, total, total_sem)
    for load in loads[0]:
        load.start()
    done.start()
    for load in sum(loads[1:], []):
        load.start()
    sums.start()
    stores = [store]
    for m in range(WAVE):
        for load in loads[m]:
            load.wait()
        if m % 2 == 0:
            wide = back[:, :, 8 * m : 8 * m + 16].astype(F32)
        rows = slice(m % 2 * 8, m % 2 * 8 + 8)
        spec[m] += legendre_back(wide[0, :, rows], wide[1, :, rows], leg[m])
        stores.append(pltpu.make_async_copy(spec.at[m], out_hbm.at[1, m], out_sem.at[m]))
        stores[-1].start()
        if m == 0:
            done.wait()
            store.start()
    sums.wait()
    whole = total[...].astype(F32)
    squares = whole * whole
    factor = jnp.minimum(F32(1.0), LIMIT / jnp.sqrt(jnp.sum(squares, keepdims=True) + 1e-06))
    g_in[:, :128] = factor * whole[0:128]
    g_in[:, 128:] = factor * whole[128:256]
    g_mid[:, :128] = factor * whole[256:512]
    g_mid[:, 128:] = factor * whole[512:768]
    g_out[...] = factor * whole[768:1024]
    g_bin[:, :128] = factor * whole[1024:1025]
    g_bin[:, 128:] = factor * whole[1025:1026]
    g_bmid[:, :128] = factor * whole[1026:1027]
    g_bmid[:, 128:] = factor * whole[1027:1028]
    for store in stores:
        store.wait()


def shards(
    cotangent, grid_state, legendre, inverse, gauss_weights, w_in, bias_in, w_mid, bias_mid, w_out
):
    table = jnp.asarray(fourier_rows(), F32).astype(BF16)
    vmem = pl.BlockSpec(memory_space=pltpu.VMEM)
    hbm = pl.BlockSpec(memory_space=pl.ANY)
    cols = TRAJ * LATS
    message = (2 * TRAJ, SP, 2 * WAVE * HALF, CHAN)
    dma = pltpu.SemaphoreType.DMA
    state_half = jax.ShapeDtypeStruct((WAVE, CHAN, COEF), F32)
    done, spec, back, total = pl.pallas_call(
        kernel,
        name="exchange",
        out_shape=(
            state_half,
            state_half,
            jax.ShapeDtypeStruct((2, *message[1:]), BF16),
            jax.ShapeDtypeStruct((ROWS, 128), BF16),
        ),
        in_specs=[hbm] * 11,
        out_specs=[hbm] * 3 + [vmem],
        scratch_shapes=[
            pltpu.VMEM((TRAJ, WAVE, CHAN, COEF), F32),
            pltpu.VMEM((TRAJ, LATS, CHAN, LONS), BF16),
            pltpu.VMEM((WAVE, DEG, LATS * SP), BF16),
            pltpu.VMEM((WAVE, 4, 32, 32), F32),
            pltpu.VMEM((1, LATS * SP), F32),
            pltpu.VMEM((CHAN, HIDDEN), BF16),
            pltpu.VMEM((1, HIDDEN), F32),
            pltpu.VMEM((HIDDEN, HIDDEN), BF16),
            pltpu.VMEM((1, HIDDEN), F32),
            pltpu.VMEM((HIDDEN, CHAN), BF16),
            pltpu.VMEM((MC, LONS), BF16),
            pltpu.VMEM((TRAJ, WAVE, CHAN, COEF), F32),
            pltpu.VMEM((WAVE, CHAN, 3 * CHAN), BF16),
            pltpu.VMEM(message, BF16),
            pltpu.VMEM(message, BF16),
            pltpu.VMEM(message, BF16),
            pltpu.VMEM((2, *message[1:]), BF16),
            pltpu.VMEM((MC * HALF, CHAN), F32),
            pltpu.VMEM((cols, HIDDEN, LONS), BF16),
            pltpu.VMEM((cols, HIDDEN, LONS), BF16),
            pltpu.VMEM((cols, HIDDEN, LONS), F32),
            pltpu.VMEM((cols, HIDDEN, LONS), F32),
            pltpu.VMEM((HIDDEN, CHAN), BF16),
            pltpu.VMEM((HIDDEN, HIDDEN), BF16),
            pltpu.VMEM((LATS * SP, 128), F32),
            pltpu.VMEM((HIDDEN, 128), F32),
            pltpu.VMEM((HIDDEN, 128), F32),
            pltpu.VMEM((ROWS, 128), F32),
            pltpu.VMEM((HIDDEN, 128), F32),
            pltpu.VMEM((HIDDEN, 128), F32),
            pltpu.VMEM((ROWS, 128), BF16),
            pltpu.VMEM((32, SEG, 128), BF16),
            pltpu.VMEM((Z, SEG, 128), BF16),
            dma((12,)),
            dma((TRAJ, WAVE)),
            dma,
            dma((2 * TRAJ,)),
            dma((2 * TRAJ,)),
            dma((2 * TRAJ,)),
            dma((2 * TRAJ,)),
            dma,
            dma,
            dma,
            dma,
            dma,
            dma,
        ],
        compiler_params=pltpu.CompilerParams(
            collective_id=0, has_side_effects=True, vmem_limit_bytes=60 * 1024 * 1024
        ),
    )(
        cotangent, grid_state, legendre, inverse, gauss_weights.reshape(1, -1),
        w_in, bias_in.reshape(1, -1), w_mid, bias_mid.reshape(1, -1), w_out, table,
    )
    state, g_in, g_bin, g_mid, g_bmid, g_out = pl.pallas_call(
        last_kernel,
        name="finish",
        out_shape=(
            jax.ShapeDtypeStruct((TRAJ, WAVE, CHAN, COEF), F32),
            jax.ShapeDtypeStruct((CHAN, HIDDEN), F32),
            jax.ShapeDtypeStruct((1, HIDDEN), F32),
            jax.ShapeDtypeStruct((HIDDEN, HIDDEN), F32),
            jax.ShapeDtypeStruct((1, HIDDEN), F32),
            jax.ShapeDtypeStruct((HIDDEN, CHAN), F32),
        ),
        in_specs=[hbm] * 5,
        out_specs=[hbm] + [vmem] * 5,
        scratch_shapes=[
            pltpu.VMEM((WAVE, CHAN, COEF), F32),
            pltpu.VMEM((WAVE, CHAN, COEF), F32),
            pltpu.VMEM((2, *message[1:]), BF16),
            pltpu.VMEM((WAVE, DEG, LATS * SP), BF16),
            pltpu.VMEM((ROWS, 128), BF16),
            dma((WAVE, 2)),
            dma((3,)),
            dma((WAVE,)),
            dma((2,)),
            dma,
        ],
        compiler_params=pltpu.CompilerParams(vmem_limit_bytes=60 * 1024 * 1024),
    )(done, spec, back, legendre, total)
    return state, g_in, g_bin.reshape(-1), g_mid, g_bmid.reshape(-1), g_out


def solution(mesh):
    return jax.shard_map(
        shards,
        mesh=mesh,
        in_specs=(
            P("batch", "space", None, None),
            P("batch", "space", None, None),
            P("space", None, None),
            P("space", None, None, None),
            P(),
            P(),
            P(),
            P(),
            P(),
            P(),
        ),
        out_specs=(P("batch", "space", None, None), P(), P(), P(), P(), P()),
        check_vma=False,
    )
```

```python
import functools
import math

import jax
import jax.numpy as jnp
import numpy as np
from jax import lax
from jax.experimental import pallas as pl
from jax.experimental.pallas import tpu as pltpu
from jax.sharding import PartitionSpec as P

MESH = pl.DeviceIdType.MESH
F32 = jnp.float32
BF16 = jnp.bfloat16

Z, X, NB = 8, 4, 8
SP = Z * X
TRAJ, WAVE, LATS = 2, 6, 8
CHAN, HIDDEN, LONS, DEG = 128, 256, 512, 192
COEF = 2 * DEG
MC = 2 * WAVE * SP
SEG = 48
ROWS = 32 * SEG
HELD = 16
LIMIT = math.sqrt(2 * CHAN * HIDDEN + HIDDEN * HIDDEN + 2 * HIDDEN)


def fourier_rows():
    waves = WAVE * SP
    phase = (np.arange(waves)[:, None] * np.arange(LONS)[None, :]) % LONS
    phase = phase * (2.0 * math.pi / LONS)
    table = np.stack([np.cos(phase), -np.sin(phase)], axis=1) / math.sqrt(waves)
    return table.reshape(MC, LONS).astype(np.float32)


def dot(a, b, ca, cb):
    return lax.dot_general(a, b, (((ca,), (cb,)), ((), ())), preferred_element_type=F32)


def column(row_ref):
    return jnp.broadcast_to(row_ref[...], (128, row_ref.shape[1])).T


def gelu_pair(v):
    square = v * v
    tanh_part = jnp.tanh(v * (0.7978845608 + 0.7978845608 * 0.044715 * square))
    up = 0.5 + 0.5 * tanh_part
    value = v * up
    bend = 0.7978845608 + 0.7978845608 * 0.134145 * square
    slope = up + 0.5 * v * (1.0 - tanh_part * tanh_part) * bend
    return value, slope


def legendre_back(back, leg):
    wide = back.astype(F32)
    real = wide[:, :LATS].reshape(LATS * SP, CHAN)
    imag = wide[:, LATS:].reshape(LATS * SP, CHAN)
    sums = dot(jnp.concatenate([real, imag], axis=1).astype(BF16), leg, 0, 1)
    return jnp.concatenate([sums[:CHAN], sums[CHAN:]], axis=1)


def sum_of(ref, count):
    first = ref[0].astype(F32)
    whole = lax.fori_loop(1, count, lambda i, t: t + ref[i].astype(F32), first)
    return whole.astype(BF16)


def kernel(
    cot_hbm, grid_hbm, leg_hbm, inv_hbm, gw_hbm, w_in_hbm, b_in_hbm, w_mid_hbm, b_mid_hbm, w_out_hbm,
    tab_hbm, done_hbm, spec_hbm, back_hbm, total_hbm,
    cot, grid, leg, inv, gw, w_in, b_in, w_mid, b_mid, w_out, tab,
    spec, solve, send1, recv1, send2, recv2, wide,
    h_in, h_mid, s_in, s_mid, w_in_t, w_mid_t, col_g, col_in, col_mid,
    acc, acc_bin, acc_bmid, parts, got_a, got_z, summed,
    in_sem, out_sem, own_sem, sum_sem, ready,
    s1_sem, r1_sem, s2_sem, r2_sem, sa_sem, ra_sem, sz_sem, rz_sem, sc_sem, rc_sem,
):
    me = lax.axis_index("space")
    bat = lax.axis_index("batch")
    z, x = lax.div(me, X), lax.rem(me, X)
    gi = bat * X + x

    loads = [
        pltpu.make_async_copy(source, target, in_sem.at[i])
        for i, (source, target) in enumerate([
            (inv_hbm, inv), (cot_hbm.at[0], cot.at[0]), (leg_hbm, leg), (gw_hbm, gw),
            (cot_hbm.at[1], cot.at[1]), (w_in_hbm, w_in), (b_in_hbm, b_in), (w_mid_hbm, w_mid),
            (b_mid_hbm, b_mid), (grid_hbm, grid), (w_out_hbm, w_out), (tab_hbm, tab),
        ])
    ]
    for load in loads[:4]:
        load.start()

    def shift(t):
        i, g = lax.rem(t, 8), lax.div(t, 8)
        return 4 + (1 - 2 * lax.rem(i, 2)) * lax.div(i + 1, 2), g + lax.div(i, 2)

    def space_peer(t):
        dz, dx = shift(t)
        return lax.rem(z + dz, Z) * X + lax.rem(x + dx, X)

    def group_peer(s):
        g = lax.rem(gi + s, 32)
        return g, (z * X + lax.rem(g, X), lax.div(g, X))

    def depth_peer(s):
        return lax.rem(z + s, Z) * X + x

    def each(first, last, act, unroll=1):
        def body(s, carry):
            act(s)
            return carry

        lax.fori_loop(first, last, body, 0, unroll=unroll)

    def peers(act, first=0, last=31):
        each(first, last, lambda t: act(t + lax.div(t + 17, 32)))

    barrier = pltpu.get_barrier_semaphore()

    def greet(t):
        pl.semaphore_signal(barrier, inc=1, device_id=(space_peer(t), bat), device_id_type=MESH)

    def greet_batch(s):
        where = (me, lax.rem(bat + s, NB))
        pl.semaphore_signal(barrier, inc=1, device_id=where, device_id_type=MESH)

    def confirm(s):
        where = (z * X + lax.rem(x + s, X), bat)
        pl.semaphore_signal(ready, inc=1, device_id=where, device_id_type=MESH)

    peers(greet)
    each(1, NB, greet_batch)

    def copy1(b, s):
        peer = space_peer(s)
        return pltpu.make_async_remote_copy(
            src_ref=send1.at[b, peer], dst_ref=recv1.at[b, me],
            send_sem=s1_sem.at[b], recv_sem=r1_sem.at[b],
            device_id=(peer, bat), device_id_type=MESH,
        )

    def copy2(b, s):
        peer = space_peer(s)
        return pltpu.make_async_remote_copy(
            src_ref=send2.at[b, peer], dst_ref=recv2.at[me] if b == 0 else back_hbm.at[me],
            send_sem=s2_sem.at[b], recv_sem=r2_sem.at[b],
            device_id=(peer, bat), device_id_type=MESH,
        )

    def copy_a(s):
        g, where = group_peer(s)
        return pltpu.make_async_remote_copy(
            src_ref=parts.at[pl.ds(pl.multiple_of(g * SEG, SEG), SEG)], dst_ref=got_a.at[gi],
            send_sem=sa_sem, recv_sem=ra_sem, device_id=where, device_id_type=MESH,
        )

    def copy_z(s):
        return pltpu.make_async_remote_copy(
            src_ref=got_z.at[z], dst_ref=got_z.at[z],
            send_sem=sz_sem, recv_sem=rz_sem,
            device_id=(depth_peer(s), bat), device_id_type=MESH,
        )

    def copy_c(s):
        _, where = group_peer(s)
        mine = pl.ds(pl.multiple_of(gi * SEG, SEG), SEG)
        return pltpu.make_async_remote_copy(
            src_ref=summed, dst_ref=total_hbm.at[mine],
            send_sem=sc_sem, recv_sem=rc_sem, device_id=where, device_id_type=MESH,
        )

    def bulk(source, target, send_sem, recv_sem):
        return pltpu.make_async_remote_copy(
            src_ref=source, dst_ref=target, send_sem=send_sem, recv_sem=recv_sem,
            device_id=(space_peer(0), bat), device_id_type=MESH,
        )

    def all1(b):
        part = pl.ds(0, SP - 1)
        return bulk(send1.at[b, part], recv1.at[b, part], s1_sem.at[b], r1_sem.at[b])

    def all2(b):
        part = pl.ds(0, SP - 1)
        target = recv2.at[part] if b == 0 else back_hbm.at[part]
        return bulk(send2.at[b, part], target, s2_sem.at[b], r2_sem.at[b])

    def all_a():
        return bulk(parts.at[pl.ds(0, 31 * SEG)], got_a.at[pl.ds(0, 31)], sa_sem, ra_sem)

    def all_z():
        return bulk(got_z.at[pl.ds(0, Z - 1)], got_z.at[pl.ds(0, Z - 1)], sz_sem, rz_sem)

    def all_c():
        part = pl.ds(0, 31 * SEG)
        return bulk(parts.at[part], total_hbm.at[part], sc_sem, rc_sem)

    lane = lax.broadcasted_iota(jnp.int32, (32, CHAN), 1)
    row = lax.broadcasted_iota(jnp.int32, (32, CHAN), 0)
    repeat = jnp.where(lane % 32 == row, 1.0, 0.0).astype(BF16)
    lane = lax.broadcasted_iota(jnp.int32, (CHAN, CHAN), 1)
    row = lax.broadcasted_iota(jnp.int32, (CHAN, CHAN), 0)
    same = lane // 32 == row // 32

    def spectral_in(b, m):
        if b == 0:
            block = inv[m].reshape(CHAN, 32)
            high = block.astype(BF16)
            low = (block - high.astype(F32)).astype(BF16)
            high = jnp.where(same, dot(high, repeat, 1, 0), 0.0).T.astype(BF16)
            low = jnp.where(same, dot(low, repeat, 1, 0), 0.0).T.astype(BF16)
            solve[m] = jnp.concatenate([high, low, high], axis=1)
        value = cot[b, m]
        value_high = value.astype(BF16)
        value_low = (value - value_high.astype(F32)).astype(BF16)
        grad = dot(
            solve[m], jnp.concatenate([value_high, value_high, value_low], axis=0), 1, 0
        )
        spec[b, m] = grad
        half = grad.astype(BF16)
        half = jnp.concatenate([half[:, :DEG], half[:, DEG:]], axis=0)
        sums = dot(leg[m], half, 0, 1)
        scaled = (sums * jnp.concatenate([col_g[...]] * 2, axis=1)).reshape(SP, LATS, 2 * CHAN)
        scaled = jnp.concatenate([scaled[:, :, :CHAN], scaled[:, :, CHAN:]], axis=1)
        send1[b, :, m] = scaled.astype(BF16)
        if b == 1:
            pltpu.make_async_copy(spec.at[1, m], spec_hbm.at[m], out_sem.at[1, m]).start()

    for load in loads[:4]:
        load.wait()
    for load in loads[4:]:
        load.start()
    col_g[...] = column(gw)
    for b in range(TRAJ):
        if b == 1:
            loads[4].wait()
        for m in range(WAVE):
            spectral_in(b, m)
        if b == 0:
            pl.semaphore_wait(barrier, SP - 1 + NB - 1)
        if b == 0:
            peers(lambda t: copy1(0, t).start())
            each(1, X, confirm)
        recv1[b, me] = send1[b, me]

    for load in loads[5:]:
        load.wait()
    w_in_t[...] = w_in[...].T
    w_mid_t[...] = w_mid[...].T
    col_in[...] = column(b_in)
    col_mid[...] = column(b_mid)
    acc[...] = jnp.zeros_like(acc)
    acc_bin[...] = jnp.zeros_like(acc_bin)
    acc_bmid[...] = jnp.zeros_like(acc_bmid)
    def forward(i):
        b, a = i // LATS, i % LATS
        first = 2 * i
        peers(lambda t: copy1(1, t).start(), first, jnp.minimum(first + 2, 31))
        pre = dot(w_in_t[...], grid[b, a], 1, 0)
        value, slope = gelu_pair(pre + jnp.concatenate([col_in[...]] * 4, axis=1))
        hidden = value.astype(BF16)
        h_in[i] = hidden
        s_in[i] = slope
        pre = dot(w_mid_t[...], hidden, 1, 0)
        value, slope = gelu_pair(pre + jnp.concatenate([col_mid[...]] * 4, axis=1))
        h_mid[i] = value.astype(BF16)
        s_mid[i] = slope

    each(0, TRAJ * LATS, forward)

    def lane_sum(v):
        return v[:, :128] + v[:, 128:256] + v[:, 256:384] + v[:, 384:]

    def backward(b, a):
        i = b * LATS + a
        part = wide[pl.ds(a, MC, stride=LATS), :].astype(BF16)
        tend = dot(part, tab[...], 0, 0).astype(BF16)
        acc[768:1024] += dot(h_mid[i], tend, 1, 1)
        err_mid = (dot(w_out[...], tend, 1, 0) * s_mid[i]).astype(BF16)
        mid = dot(h_in[i], err_mid, 1, 1)
        acc[256:512] += mid[:, :128]
        acc[512:768] += mid[:, 128:]
        acc_bmid[...] += lane_sum(err_mid.astype(F32))
        err_in = (dot(w_mid[...], err_mid, 1, 0) * s_in[i]).astype(BF16)
        raw = dot(grid[b, a], err_in, 1, 1)
        acc[0:128] += raw[:, :128]
        acc[128:256] += raw[:, 128:]
        acc_bin[...] += lane_sum(err_in.astype(F32))
        state = dot(w_in[...], err_in, 1, 0).astype(BF16)
        wide[pl.ds(a, MC, stride=LATS), :] = dot(tab[...], state, 1, 1)

    per_peer = 2 * WAVE * LATS

    def unpack(b, peer):
        rows = pl.ds(pl.multiple_of(peer * per_peer, per_peer), per_peer)
        wide[rows, :] = recv1[b, peer].reshape(per_peer, CHAN).astype(F32)

    def pack(b, peer):
        rows = pl.ds(pl.multiple_of(peer * per_peer, per_peer), per_peer)
        send2[b, peer] = wide[rows, :].astype(BF16).reshape(WAVE, 2 * LATS, CHAN)

    for b in range(TRAJ):
        all1(b).wait_recv()
        each(0, SP, functools.partial(unpack, b), 4)
        each(0, LATS, functools.partial(backward, b), 4)

        def depart(t):
            pack(b, space_peer(t))
            copy2(b, t).start()

        if b == 0:
            peers(depart)
            pack(b, me)
            recv2[me] = send2[b, me]

    bins = jnp.sum(acc_bin[...].T, axis=0, keepdims=True)
    bmids = jnp.sum(acc_bmid[...].T, axis=0, keepdims=True)
    acc[1024:1025] = bins[:, :128]
    acc[1025:1026] = bins[:, 128:]
    acc[1026:1027] = bmids[:, :128]
    acc[1027:1028] = bmids[:, 128:]
    parts[...] = acc[...].astype(BF16)
    pl.semaphore_wait(ready, X - 1)
    each(1, 32, lambda s: copy_a(s).start())
    peers(depart, 0, HELD)
    pack(1, me)
    own = pltpu.make_async_copy(send2.at[1, me], back_hbm.at[me], own_sem)
    own.start()
    mine = pl.ds(pl.multiple_of(gi * SEG, SEG), SEG)
    got_a[gi] = parts[mine]
    all_a().wait_recv()
    got_z[z] = sum_of(got_a, 32)
    each(1, Z, lambda s: copy_z(s).start())
    peers(depart, HELD, 31)

    def finish(m):
        spec[0, m] += legendre_back(recv2[:, m], leg[m])
        pltpu.make_async_copy(spec.at[0, m], done_hbm.at[m], out_sem.at[0, m]).start()

    all2(0).wait_recv()
    for m in range(WAVE):
        finish(m)
    all_z().wait_recv()
    summed[...] = sum_of(got_z, Z)
    own_sum = pltpu.make_async_copy(summed, total_hbm.at[mine], sum_sem)
    own_sum.start()
    each(1, 32, lambda s: copy_c(s).start())
    own.wait()
    own_sum.wait()
    for b in range(TRAJ):
        all1(b).wait_send()
        all2(b).wait_send()
    for m in range(WAVE):
        pltpu.make_async_copy(spec.at[0, m], done_hbm.at[m], out_sem.at[0, m]).wait()
        pltpu.make_async_copy(spec.at[1, m], spec_hbm.at[m], out_sem.at[1, m]).wait()
    all_a().wait_send()
    all_z().wait_send()
    all_c().wait_recv()
    all_c().wait_send()
    all2(1).wait_recv()


def last_kernel(
    done_hbm, spec_hbm, back_hbm, leg_hbm, total_hbm,
    out_hbm, in_hbm, bin_hbm, mid_hbm, bmid_hbm, wout_hbm,
    g_in, g_bin, g_mid, g_bmid, g_out, held, spec, back, leg, total,
    sem, out_sem, done_sem, total_sem, grad_sem,
):
    done = pltpu.make_async_copy(done_hbm, held, done_sem.at[0])
    stores = [pltpu.make_async_copy(held, out_hbm.at[0], done_sem.at[1])]
    loads = [
        [
            pltpu.make_async_copy(back_hbm.at[:, m], back.at[:, m], sem.at[m, 0]),
            pltpu.make_async_copy(leg_hbm.at[m], leg.at[m], sem.at[m, 1]),
            pltpu.make_async_copy(spec_hbm.at[m], spec.at[m], sem.at[m, 2]),
        ]
        for m in range(WAVE)
    ]
    sums = pltpu.make_async_copy(total_hbm, total, total_sem)
    sums.start()
    for load in sum(loads, []):
        load.start()
    done.start()
    sums.wait()
    whole = total[...].astype(F32)
    squares = whole * whole
    factor = jnp.minimum(F32(1.0), LIMIT / jnp.sqrt(jnp.sum(squares, keepdims=True) + 1e-06))
    g_in[:, :128] = factor * whole[0:128]
    g_in[:, 128:] = factor * whole[128:256]
    g_mid[:, :128] = factor * whole[256:512]
    g_mid[:, 128:] = factor * whole[512:768]
    g_out[...] = factor * whole[768:1024]
    g_bin[:, :128] = factor * whole[1024:1025]
    g_bin[:, 128:] = factor * whole[1025:1026]
    g_bmid[:, :128] = factor * whole[1026:1027]
    g_bmid[:, 128:] = factor * whole[1027:1028]
    for i, (source, target) in enumerate([
        (g_in, in_hbm), (g_bin, bin_hbm), (g_mid, mid_hbm), (g_bmid, bmid_hbm), (g_out, wout_hbm),
    ]):
        stores.append(pltpu.make_async_copy(source, target, grad_sem.at[i]))
        stores[-1].start()
    for m in range(WAVE):
        for load in loads[m]:
            load.wait()
        spec[m] += legendre_back(back[:, m], leg[m])
        stores.append(pltpu.make_async_copy(spec.at[m], out_hbm.at[1, m], out_sem.at[m]))
        stores[-1].start()
        if m == 1:
            done.wait()
            stores[0].start()
    for store in stores:
        store.wait()


def shards(
    cotangent, grid_state, legendre, inverse, gauss_weights, w_in, bias_in, w_mid, bias_mid, w_out
):
    table = jnp.asarray(fourier_rows(), F32).astype(BF16)
    hbm = pl.BlockSpec(memory_space=pl.ANY)
    cols = TRAJ * LATS
    message = (TRAJ, SP, WAVE, 2 * LATS, CHAN)
    dma = pltpu.SemaphoreType.DMA
    state_half = jax.ShapeDtypeStruct((WAVE, CHAN, COEF), F32)
    done, spec, back, total = pl.pallas_call(
        kernel,
        name="exchange",
        out_shape=(
            state_half,
            state_half,
            jax.ShapeDtypeStruct(message[1:], BF16),
            jax.ShapeDtypeStruct((ROWS, 128), BF16),
        ),
        in_specs=[hbm] * 11,
        out_specs=[hbm] * 4,
        scratch_shapes=[
            pltpu.VMEM((TRAJ, WAVE, CHAN, COEF), F32),
            pltpu.VMEM((TRAJ, LATS, CHAN, LONS), BF16),
            pltpu.VMEM((WAVE, DEG, LATS * SP), BF16),
            pltpu.VMEM((WAVE, 4, 32, 32), F32),
            pltpu.VMEM((1, LATS * SP), F32),
            pltpu.VMEM((CHAN, HIDDEN), BF16),
            pltpu.VMEM((1, HIDDEN), F32),
            pltpu.VMEM((HIDDEN, HIDDEN), BF16),
            pltpu.VMEM((1, HIDDEN), F32),
            pltpu.VMEM((HIDDEN, CHAN), BF16),
            pltpu.VMEM((MC, LONS), BF16),
            pltpu.VMEM((TRAJ, WAVE, CHAN, COEF), F32),
            pltpu.VMEM((WAVE, CHAN, 3 * CHAN), BF16),
            pltpu.VMEM(message, BF16),
            pltpu.VMEM(message, BF16),
            pltpu.VMEM(message, BF16),
            pltpu.VMEM(message[1:], BF16),
            pltpu.VMEM((MC * LATS, CHAN), F32),
            pltpu.VMEM((cols, HIDDEN, LONS), BF16),
            pltpu.VMEM((cols, HIDDEN, LONS), BF16),
            pltpu.VMEM((cols, HIDDEN, LONS), F32),
            pltpu.VMEM((cols, HIDDEN, LONS), F32),
            pltpu.VMEM((HIDDEN, CHAN), BF16),
            pltpu.VMEM((HIDDEN, HIDDEN), BF16),
            pltpu.VMEM((LATS * SP, 128), F32),
            pltpu.VMEM((HIDDEN, 128), F32),
            pltpu.VMEM((HIDDEN, 128), F32),
            pltpu.VMEM((ROWS, 128), F32),
            pltpu.VMEM((HIDDEN, 128), F32),
            pltpu.VMEM((HIDDEN, 128), F32),
            pltpu.VMEM((ROWS, 128), BF16),
            pltpu.VMEM((32, SEG, 128), BF16),
            pltpu.VMEM((Z, SEG, 128), BF16),
            pltpu.VMEM((SEG, 128), BF16),
            dma((12,)),
            dma((TRAJ, WAVE)),
            dma,
            dma,
            pltpu.SemaphoreType.REGULAR,
            dma((TRAJ,)),
            dma((TRAJ,)),
            dma((TRAJ,)),
            dma((TRAJ,)),
            dma,
            dma,
            dma,
            dma,
            dma,
            dma,
        ],
        compiler_params=pltpu.CompilerParams(
            collective_id=0, has_side_effects=True, vmem_limit_bytes=60 * 1024 * 1024
        ),
    )(
        cotangent, grid_state, legendre, inverse, gauss_weights.reshape(1, -1),
        w_in, bias_in.reshape(1, -1), w_mid, bias_mid.reshape(1, -1), w_out, table,
    )
    state, g_in, g_bin, g_mid, g_bmid, g_out = pl.pallas_call(
        last_kernel,
        name="finish",
        out_shape=(
            jax.ShapeDtypeStruct((TRAJ, WAVE, CHAN, COEF), F32),
            jax.ShapeDtypeStruct((CHAN, HIDDEN), F32),
            jax.ShapeDtypeStruct((1, HIDDEN), F32),
            jax.ShapeDtypeStruct((HIDDEN, HIDDEN), F32),
            jax.ShapeDtypeStruct((1, HIDDEN), F32),
            jax.ShapeDtypeStruct((HIDDEN, CHAN), F32),
        ),
        in_specs=[hbm] * 5,
        out_specs=[hbm] * 6,
        scratch_shapes=[
            pltpu.VMEM((CHAN, HIDDEN), F32),
            pltpu.VMEM((1, HIDDEN), F32),
            pltpu.VMEM((HIDDEN, HIDDEN), F32),
            pltpu.VMEM((1, HIDDEN), F32),
            pltpu.VMEM((HIDDEN, CHAN), F32),
            pltpu.VMEM((WAVE, CHAN, COEF), F32),
            pltpu.VMEM((WAVE, CHAN, COEF), F32),
            pltpu.VMEM(message[1:], BF16),
            pltpu.VMEM((WAVE, DEG, LATS * SP), BF16),
            pltpu.VMEM((ROWS, 128), BF16),
            dma((WAVE, 3)),
            dma((WAVE,)),
            dma((2,)),
            dma,
            dma((5,)),
        ],
        compiler_params=pltpu.CompilerParams(vmem_limit_bytes=60 * 1024 * 1024),
    )(done, spec, back, legendre, total)
    return state, g_in, g_bin.reshape(-1), g_mid, g_bmid.reshape(-1), g_out


def solution(mesh):
    return jax.shard_map(
        shards,
        mesh=mesh,
        in_specs=(
            P("batch", "space", None, None),
            P("batch", "space", None, None),
            P("space", None, None),
            P("space", None, None, None),
            P(),
            P(),
            P(),
            P(),
            P(),
            P(),
        ),
        out_specs=(P("batch", "space", None, None), P(), P(), P(), P(), P()),
        check_vma=False,
    )
```

```python
import functools
import math

import jax
import jax.numpy as jnp
import numpy as np
from jax import lax
from jax.experimental import pallas as pl
from jax.experimental.pallas import tpu as pltpu
from jax.sharding import PartitionSpec as P

MESH = pl.DeviceIdType.MESH
F32 = jnp.float32
BF16 = jnp.bfloat16

Z, X, NB = 8, 4, 8
SP = Z * X
TRAJ, WAVE, LATS = 2, 6, 8
CHAN, HIDDEN, LONS, DEG = 128, 256, 512, 192
COEF = 2 * DEG
MC = 2 * WAVE * SP
SEG = 48
ROWS = 32 * SEG
HELD = 8
LIMIT = math.sqrt(2 * CHAN * HIDDEN + HIDDEN * HIDDEN + 2 * HIDDEN)


def fourier_rows():
    waves = WAVE * SP
    phase = (np.arange(waves)[:, None] * np.arange(LONS)[None, :]) % LONS
    phase = phase * (2.0 * math.pi / LONS)
    table = np.stack([np.cos(phase), -np.sin(phase)], axis=1) / math.sqrt(waves)
    return table.reshape(MC, LONS).astype(np.float32)


def dot(a, b, ca, cb):
    return lax.dot_general(a, b, (((ca,), (cb,)), ((), ())), preferred_element_type=F32)


def column(row_ref):
    return jnp.broadcast_to(row_ref[...], (128, row_ref.shape[1])).T


def gelu_pair(v):
    square = v * v
    tanh_part = jnp.tanh(v * (0.7978845608 + 0.7978845608 * 0.044715 * square))
    up = 0.5 + 0.5 * tanh_part
    value = v * up
    bend = 0.7978845608 + 0.7978845608 * 0.134145 * square
    slope = up + 0.5 * v * (1.0 - tanh_part * tanh_part) * bend
    return value, slope


def legendre_back(back, leg):
    wide = back.astype(F32)
    real = wide[:, :LATS].reshape(LATS * SP, CHAN)
    imag = wide[:, LATS:].reshape(LATS * SP, CHAN)
    sums = dot(jnp.concatenate([real, imag], axis=1).astype(BF16), leg, 0, 1)
    return jnp.concatenate([sums[:CHAN], sums[CHAN:]], axis=1)


def sum_of(ref, count):
    first = ref[0].astype(F32)
    whole = lax.fori_loop(1, count, lambda i, t: t + ref[i].astype(F32), first)
    return whole.astype(BF16)


def kernel(
    cot_hbm, grid_hbm, leg_hbm, inv_hbm, gw_hbm, w_in_hbm, b_in_hbm, w_mid_hbm, b_mid_hbm, w_out_hbm,
    tab_hbm, done_hbm, spec_hbm, back_hbm, total_hbm,
    cot, grid, leg, inv, gw, w_in, b_in, w_mid, b_mid, w_out, tab,
    spec, solve, send1, recv1, send2, recv2, wide,
    h_in, h_mid, s_in, s_mid, w_in_t, w_mid_t, col_g, col_in, col_mid,
    acc, acc_bin, acc_bmid, parts, got_a, got_z, summed,
    in_sem, out_sem, own_sem, sum_sem, ready,
    s1_sem, r1_sem, s2_sem, r2_sem, sa_sem, ra_sem, sz_sem, rz_sem, sc_sem, rc_sem,
):
    me = lax.axis_index("space")
    bat = lax.axis_index("batch")
    z, x = lax.div(me, X), lax.rem(me, X)
    gi = bat * X + x

    loads = [
        pltpu.make_async_copy(source, target, in_sem.at[i])
        for i, (source, target) in enumerate([
            (inv_hbm, inv), (cot_hbm.at[0], cot.at[0]), (leg_hbm, leg), (gw_hbm, gw),
            (cot_hbm.at[1], cot.at[1]), (w_in_hbm, w_in), (b_in_hbm, b_in), (w_mid_hbm, w_mid),
            (b_mid_hbm, b_mid), (grid_hbm, grid), (w_out_hbm, w_out), (tab_hbm, tab),
        ])
    ]
    for load in loads[:4]:
        load.start()

    def shift(t):
        i, g = lax.rem(t, 8), lax.div(t, 8)
        return 4 + (1 - 2 * lax.rem(i, 2)) * lax.div(i + 1, 2), g + lax.div(i, 2)

    def space_peer(t):
        dz, dx = shift(t)
        return lax.rem(z + dz, Z) * X + lax.rem(x + dx, X)

    def group_peer(s):
        g = lax.rem(gi + s, 32)
        return g, (z * X + lax.rem(g, X), lax.div(g, X))

    def depth_peer(s):
        return lax.rem(z + s, Z) * X + x

    def each(first, last, act, unroll=1):
        def body(s, carry):
            act(s)
            return carry

        lax.fori_loop(first, last, body, 0, unroll=unroll)

    def peers(act, first=0, last=31):
        each(first, last, lambda t: act(t + lax.div(t + 17, 32)))

    barrier = pltpu.get_barrier_semaphore()

    def greet(t):
        pl.semaphore_signal(barrier, inc=1, device_id=(space_peer(t), bat), device_id_type=MESH)

    def greet_batch(s):
        where = (me, lax.rem(bat + s, NB))
        pl.semaphore_signal(barrier, inc=1, device_id=where, device_id_type=MESH)

    def confirm(s):
        where = (z * X + lax.rem(x + s, X), bat)
        pl.semaphore_signal(ready, inc=1, device_id=where, device_id_type=MESH)

    peers(greet)
    each(1, NB, greet_batch)

    def copy1(b, s):
        peer = space_peer(s)
        return pltpu.make_async_remote_copy(
            src_ref=send1.at[b, peer], dst_ref=recv1.at[b, me],
            send_sem=s1_sem.at[b], recv_sem=r1_sem.at[b],
            device_id=(peer, bat), device_id_type=MESH,
        )

    def copy2(b, s):
        peer = space_peer(s)
        return pltpu.make_async_remote_copy(
            src_ref=send2.at[b, peer], dst_ref=recv2.at[me] if b == 0 else back_hbm.at[me],
            send_sem=s2_sem.at[b], recv_sem=r2_sem.at[b],
            device_id=(peer, bat), device_id_type=MESH,
        )

    def copy_a(s):
        g, where = group_peer(s)
        return pltpu.make_async_remote_copy(
            src_ref=parts.at[pl.ds(pl.multiple_of(g * SEG, SEG), SEG)], dst_ref=got_a.at[gi],
            send_sem=sa_sem, recv_sem=ra_sem, device_id=where, device_id_type=MESH,
        )

    def copy_z(s):
        return pltpu.make_async_remote_copy(
            src_ref=got_z.at[z], dst_ref=got_z.at[z],
            send_sem=sz_sem, recv_sem=rz_sem,
            device_id=(depth_peer(s), bat), device_id_type=MESH,
        )

    def copy_c(s):
        _, where = group_peer(s)
        mine = pl.ds(pl.multiple_of(gi * SEG, SEG), SEG)
        return pltpu.make_async_remote_copy(
            src_ref=summed, dst_ref=total_hbm.at[mine],
            send_sem=sc_sem, recv_sem=rc_sem, device_id=where, device_id_type=MESH,
        )

    def bulk(source, target, send_sem, recv_sem):
        return pltpu.make_async_remote_copy(
            src_ref=source, dst_ref=target, send_sem=send_sem, recv_sem=recv_sem,
            device_id=(space_peer(0), bat), device_id_type=MESH,
        )

    def all1(b):
        part = pl.ds(0, SP - 1)
        return bulk(send1.at[b, part], recv1.at[b, part], s1_sem.at[b], r1_sem.at[b])

    def all2(b):
        part = pl.ds(0, SP - 1)
        target = recv2.at[part] if b == 0 else back_hbm.at[part]
        return bulk(send2.at[b, part], target, s2_sem.at[b], r2_sem.at[b])

    def all_a():
        return bulk(parts.at[pl.ds(0, 31 * SEG)], got_a.at[pl.ds(0, 31)], sa_sem, ra_sem)

    def all_z():
        return bulk(got_z.at[pl.ds(0, Z - 1)], got_z.at[pl.ds(0, Z - 1)], sz_sem, rz_sem)

    def all_c():
        part = pl.ds(0, 31 * SEG)
        return bulk(parts.at[part], total_hbm.at[part], sc_sem, rc_sem)

    lane = lax.broadcasted_iota(jnp.int32, (32, CHAN), 1)
    row = lax.broadcasted_iota(jnp.int32, (32, CHAN), 0)
    repeat = jnp.where(lane % 32 == row, 1.0, 0.0).astype(BF16)
    lane = lax.broadcasted_iota(jnp.int32, (CHAN, CHAN), 1)
    row = lax.broadcasted_iota(jnp.int32, (CHAN, CHAN), 0)
    same = lane // 32 == row // 32

    def spectral_in(b, m):
        if b == 0:
            block = inv[m].reshape(CHAN, 32)
            high = block.astype(BF16)
            low = (block - high.astype(F32)).astype(BF16)
            high = jnp.where(same, dot(high, repeat, 1, 0), 0.0).T.astype(BF16)
            low = jnp.where(same, dot(low, repeat, 1, 0), 0.0).T.astype(BF16)
            solve[m] = jnp.concatenate([high, low, high], axis=1)
        value = cot[b, m]
        value_high = value.astype(BF16)
        value_low = (value - value_high.astype(F32)).astype(BF16)
        grad = dot(
            solve[m], jnp.concatenate([value_high, value_high, value_low], axis=0), 1, 0
        )
        spec[b, m] = grad
        half = grad.astype(BF16)
        half = jnp.concatenate([half[:, :DEG], half[:, DEG:]], axis=0)
        sums = dot(leg[m], half, 0, 1)
        scaled = (sums * jnp.concatenate([col_g[...]] * 2, axis=1)).reshape(SP, LATS, 2 * CHAN)
        scaled = jnp.concatenate([scaled[:, :, :CHAN], scaled[:, :, CHAN:]], axis=1)
        send1[b, :, m] = scaled.astype(BF16)
        if b == 1:
            pltpu.make_async_copy(spec.at[1, m], spec_hbm.at[m], out_sem.at[1, m]).start()

    for load in loads[:4]:
        load.wait()
    for load in loads[4:]:
        load.start()
    col_g[...] = column(gw)
    for b in range(TRAJ):
        if b == 1:
            loads[4].wait()
        for m in range(WAVE):
            spectral_in(b, m)
        if b == 0:
            pl.semaphore_wait(barrier, SP - 1 + NB - 1)
        if b == 0:
            peers(lambda t: copy1(0, t).start())
            each(1, X, confirm)
        recv1[b, me] = send1[b, me]

    for load in loads[5:]:
        load.wait()
    w_in_t[...] = w_in[...].T
    w_mid_t[...] = w_mid[...].T
    col_in[...] = column(b_in)
    col_mid[...] = column(b_mid)
    acc[...] = jnp.zeros_like(acc)
    acc_bin[...] = jnp.zeros_like(acc_bin)
    acc_bmid[...] = jnp.zeros_like(acc_bmid)
    def forward(i):
        b, a = i // LATS, i % LATS
        first = 2 * i
        peers(lambda t: copy1(1, t).start(), first, jnp.minimum(first + 2, 31))
        pre = dot(w_in_t[...], grid[b, a], 1, 0)
        value, slope = gelu_pair(pre + jnp.concatenate([col_in[...]] * 4, axis=1))
        hidden = value.astype(BF16)
        h_in[i] = hidden
        s_in[i] = slope
        pre = dot(w_mid_t[...], hidden, 1, 0)
        value, slope = gelu_pair(pre + jnp.concatenate([col_mid[...]] * 4, axis=1))
        h_mid[i] = value.astype(BF16)
        s_mid[i] = slope

    each(0, TRAJ * LATS, forward)

    def lane_sum(v):
        return v[:, :128] + v[:, 128:256] + v[:, 256:384] + v[:, 384:]

    def backward(b, a):
        i = b * LATS + a
        part = wide[pl.ds(a, MC, stride=LATS), :].astype(BF16)
        tend = dot(part, tab[...], 0, 0).astype(BF16)
        acc[768:1024] += dot(h_mid[i], tend, 1, 1)
        err_mid = (dot(w_out[...], tend, 1, 0) * s_mid[i]).astype(BF16)
        mid = dot(h_in[i], err_mid, 1, 1)
        acc[256:512] += mid[:, :128]
        acc[512:768] += mid[:, 128:]
        acc_bmid[...] += lane_sum(err_mid.astype(F32))
        err_in = (dot(w_mid[...], err_mid, 1, 0) * s_in[i]).astype(BF16)
        raw = dot(grid[b, a], err_in, 1, 1)
        acc[0:128] += raw[:, :128]
        acc[128:256] += raw[:, 128:]
        acc_bin[...] += lane_sum(err_in.astype(F32))
        state = dot(w_in[...], err_in, 1, 0).astype(BF16)
        wide[pl.ds(a, MC, stride=LATS), :] = dot(tab[...], state, 1, 1)

    per_peer = 2 * WAVE * LATS

    def unpack(b, peer):
        rows = pl.ds(pl.multiple_of(peer * per_peer, per_peer), per_peer)
        wide[rows, :] = recv1[b, peer].reshape(per_peer, CHAN).astype(F32)

    def pack(b, peer):
        rows = pl.ds(pl.multiple_of(peer * per_peer, per_peer), per_peer)
        send2[b, peer] = wide[rows, :].astype(BF16).reshape(WAVE, 2 * LATS, CHAN)

    for b in range(TRAJ):
        all1(b).wait_recv()
        each(0, SP, functools.partial(unpack, b), 4)
        each(0, LATS, functools.partial(backward, b), 4)

        def depart(t):
            pack(b, space_peer(t))
            copy2(b, t).start()

        if b == 0:
            peers(depart)
            pack(b, me)
            recv2[me] = send2[b, me]

    bins = jnp.sum(acc_bin[...].T, axis=0, keepdims=True)
    bmids = jnp.sum(acc_bmid[...].T, axis=0, keepdims=True)
    acc[1024:1025] = bins[:, :128]
    acc[1025:1026] = bins[:, 128:]
    acc[1026:1027] = bmids[:, :128]
    acc[1027:1028] = bmids[:, 128:]
    parts[...] = acc[...].astype(BF16)
    pl.semaphore_wait(ready, X - 1)
    each(1, 32, lambda s: copy_a(s).start())
    peers(depart, 0, HELD)
    pack(1, me)
    own = pltpu.make_async_copy(send2.at[1, me], back_hbm.at[me], own_sem)
    own.start()
    mine = pl.ds(pl.multiple_of(gi * SEG, SEG), SEG)
    got_a[gi] = parts[mine]
    all_a().wait_recv()
    got_z[z] = sum_of(got_a, 32)
    each(1, Z, lambda s: copy_z(s).start())
    peers(depart, HELD, 31)

    def finish(m):
        spec[0, m] += legendre_back(recv2[:, m], leg[m])
        pltpu.make_async_copy(spec.at[0, m], done_hbm.at[m], out_sem.at[0, m]).start()

    all_z().wait_recv()
    summed[...] = sum_of(got_z, Z)
    own_sum = pltpu.make_async_copy(summed, total_hbm.at[mine], sum_sem)
    own_sum.start()
    each(1, 32, lambda s: copy_c(s).start())
    all2(0).wait_recv()
    for m in range(WAVE):
        finish(m)
    own.wait()
    own_sum.wait()
    for b in range(TRAJ):
        all1(b).wait_send()
        all2(b).wait_send()
    for m in range(WAVE):
        pltpu.make_async_copy(spec.at[0, m], done_hbm.at[m], out_sem.at[0, m]).wait()
        pltpu.make_async_copy(spec.at[1, m], spec_hbm.at[m], out_sem.at[1, m]).wait()
    all_a().wait_send()
    all_z().wait_send()
    all_c().wait_recv()
    all_c().wait_send()
    all2(1).wait_recv()


def last_kernel(
    done_hbm, spec_hbm, back_hbm, leg_hbm, total_hbm,
    out_hbm, in_hbm, bin_hbm, mid_hbm, bmid_hbm, wout_hbm,
    g_in, g_bin, g_mid, g_bmid, g_out, held, spec, back, leg, total,
    sem, out_sem, done_sem, total_sem, grad_sem,
):
    done = pltpu.make_async_copy(done_hbm, held, done_sem.at[0])
    stores = [pltpu.make_async_copy(held, out_hbm.at[0], done_sem.at[1])]
    loads = [
        [
            pltpu.make_async_copy(back_hbm.at[:, m], back.at[:, m], sem.at[m, 0]),
            pltpu.make_async_copy(leg_hbm.at[m], leg.at[m], sem.at[m, 1]),
            pltpu.make_async_copy(spec_hbm.at[m], spec.at[m], sem.at[m, 2]),
        ]
        for m in range(WAVE)
    ]
    sums = pltpu.make_async_copy(total_hbm, total, total_sem)
    sums.start()
    for load in sum(loads, []):
        load.start()
    done.start()
    sums.wait()
    whole = total[...].astype(F32)
    squares = whole * whole
    factor = jnp.minimum(F32(1.0), LIMIT / jnp.sqrt(jnp.sum(squares, keepdims=True) + 1e-06))
    g_in[:, :128] = factor * whole[0:128]
    g_in[:, 128:] = factor * whole[128:256]
    g_mid[:, :128] = factor * whole[256:512]
    g_mid[:, 128:] = factor * whole[512:768]
    g_out[...] = factor * whole[768:1024]
    g_bin[:, :128] = factor * whole[1024:1025]
    g_bin[:, 128:] = factor * whole[1025:1026]
    g_bmid[:, :128] = factor * whole[1026:1027]
    g_bmid[:, 128:] = factor * whole[1027:1028]
    for i, (source, target) in enumerate([
        (g_in, in_hbm), (g_bin, bin_hbm), (g_mid, mid_hbm), (g_bmid, bmid_hbm), (g_out, wout_hbm),
    ]):
        stores.append(pltpu.make_async_copy(source, target, grad_sem.at[i]))
        stores[-1].start()
    for m in range(WAVE):
        for load in loads[m]:
            load.wait()
        spec[m] += legendre_back(back[:, m], leg[m])
        stores.append(pltpu.make_async_copy(spec.at[m], out_hbm.at[1, m], out_sem.at[m]))
        stores[-1].start()
        if m == 1:
            done.wait()
            stores[0].start()
    for store in stores:
        store.wait()


def shards(
    cotangent, grid_state, legendre, inverse, gauss_weights, w_in, bias_in, w_mid, bias_mid, w_out
):
    table = jnp.asarray(fourier_rows(), F32).astype(BF16)
    hbm = pl.BlockSpec(memory_space=pl.ANY)
    cols = TRAJ * LATS
    message = (TRAJ, SP, WAVE, 2 * LATS, CHAN)
    dma = pltpu.SemaphoreType.DMA
    state_half = jax.ShapeDtypeStruct((WAVE, CHAN, COEF), F32)
    done, spec, back, total = pl.pallas_call(
        kernel,
        name="exchange",
        out_shape=(
            state_half,
            state_half,
            jax.ShapeDtypeStruct(message[1:], BF16),
            jax.ShapeDtypeStruct((ROWS, 128), BF16),
        ),
        in_specs=[hbm] * 11,
        out_specs=[hbm] * 4,
        scratch_shapes=[
            pltpu.VMEM((TRAJ, WAVE, CHAN, COEF), F32),
            pltpu.VMEM((TRAJ, LATS, CHAN, LONS), BF16),
            pltpu.VMEM((WAVE, DEG, LATS * SP), BF16),
            pltpu.VMEM((WAVE, 4, 32, 32), F32),
            pltpu.VMEM((1, LATS * SP), F32),
            pltpu.VMEM((CHAN, HIDDEN), BF16),
            pltpu.VMEM((1, HIDDEN), F32),
            pltpu.VMEM((HIDDEN, HIDDEN), BF16),
            pltpu.VMEM((1, HIDDEN), F32),
            pltpu.VMEM((HIDDEN, CHAN), BF16),
            pltpu.VMEM((MC, LONS), BF16),
            pltpu.VMEM((TRAJ, WAVE, CHAN, COEF), F32),
            pltpu.VMEM((WAVE, CHAN, 3 * CHAN), BF16),
            pltpu.VMEM(message, BF16),
            pltpu.VMEM(message, BF16),
            pltpu.VMEM(message, BF16),
            pltpu.VMEM(message[1:], BF16),
            pltpu.VMEM((MC * LATS, CHAN), F32),
            pltpu.VMEM((cols, HIDDEN, LONS), BF16),
            pltpu.VMEM((cols, HIDDEN, LONS), BF16),
            pltpu.VMEM((cols, HIDDEN, LONS), F32),
            pltpu.VMEM((cols, HIDDEN, LONS), F32),
            pltpu.VMEM((HIDDEN, CHAN), BF16),
            pltpu.VMEM((HIDDEN, HIDDEN), BF16),
            pltpu.VMEM((LATS * SP, 128), F32),
            pltpu.VMEM((HIDDEN, 128), F32),
            pltpu.VMEM((HIDDEN, 128), F32),
            pltpu.VMEM((ROWS, 128), F32),
            pltpu.VMEM((HIDDEN, 128), F32),
            pltpu.VMEM((HIDDEN, 128), F32),
            pltpu.VMEM((ROWS, 128), BF16),
            pltpu.VMEM((32, SEG, 128), BF16),
            pltpu.VMEM((Z, SEG, 128), BF16),
            pltpu.VMEM((SEG, 128), BF16),
            dma((12,)),
            dma((TRAJ, WAVE)),
            dma,
            dma,
            pltpu.SemaphoreType.REGULAR,
            dma((TRAJ,)),
            dma((TRAJ,)),
            dma((TRAJ,)),
            dma((TRAJ,)),
            dma,
            dma,
            dma,
            dma,
            dma,
            dma,
        ],
        compiler_params=pltpu.CompilerParams(
            collective_id=0, has_side_effects=True, vmem_limit_bytes=60 * 1024 * 1024
        ),
    )(
        cotangent, grid_state, legendre, inverse, gauss_weights.reshape(1, -1),
        w_in, bias_in.reshape(1, -1), w_mid, bias_mid.reshape(1, -1), w_out, table,
    )
    state, g_in, g_bin, g_mid, g_bmid, g_out = pl.pallas_call(
        last_kernel,
        name="finish",
        out_shape=(
            jax.ShapeDtypeStruct((TRAJ, WAVE, CHAN, COEF), F32),
            jax.ShapeDtypeStruct((CHAN, HIDDEN), F32),
            jax.ShapeDtypeStruct((1, HIDDEN), F32),
            jax.ShapeDtypeStruct((HIDDEN, HIDDEN), F32),
            jax.ShapeDtypeStruct((1, HIDDEN), F32),
            jax.ShapeDtypeStruct((HIDDEN, CHAN), F32),
        ),
        in_specs=[hbm] * 5,
        out_specs=[hbm] * 6,
        scratch_shapes=[
            pltpu.VMEM((CHAN, HIDDEN), F32),
            pltpu.VMEM((1, HIDDEN), F32),
            pltpu.VMEM((HIDDEN, HIDDEN), F32),
            pltpu.VMEM((1, HIDDEN), F32),
            pltpu.VMEM((HIDDEN, CHAN), F32),
            pltpu.VMEM((WAVE, CHAN, COEF), F32),
            pltpu.VMEM((WAVE, CHAN, COEF), F32),
            pltpu.VMEM(message[1:], BF16),
            pltpu.VMEM((WAVE, DEG, LATS * SP), BF16),
            pltpu.VMEM((ROWS, 128), BF16),
            dma((WAVE, 3)),
            dma((WAVE,)),
            dma((2,)),
            dma,
            dma((5,)),
        ],
        compiler_params=pltpu.CompilerParams(vmem_limit_bytes=60 * 1024 * 1024),
    )(done, spec, back, legendre, total)
    return state, g_in, g_bin.reshape(-1), g_mid, g_bmid.reshape(-1), g_out


def solution(mesh):
    return jax.shard_map(
        shards,
        mesh=mesh,
        in_specs=(
            P("batch", "space", None, None),
            P("batch", "space", None, None),
            P("space", None, None),
            P("space", None, None, None),
            P(),
            P(),
            P(),
            P(),
            P(),
            P(),
        ),
        out_specs=(P("batch", "space", None, None), P(), P(), P(), P(), P()),
        check_vma=False,
    )
```

```python
import functools
import math

import jax
import jax.numpy as jnp
import numpy as np
from jax import lax
from jax.experimental import pallas as pl
from jax.experimental.pallas import tpu as pltpu
from jax.sharding import PartitionSpec as P

MESH = pl.DeviceIdType.MESH
F32 = jnp.float32
BF16 = jnp.bfloat16

Z, X, NB = 8, 4, 8
SP = Z * X
TRAJ, WAVE, LATS = 2, 6, 8
CHAN, HIDDEN, LONS, DEG = 128, 256, 512, 192
COEF = 2 * DEG
MC = 2 * WAVE * SP
SEG = 48
ROWS = 32 * SEG
HELD = 10
LIMIT = math.sqrt(2 * CHAN * HIDDEN + HIDDEN * HIDDEN + 2 * HIDDEN)


def fourier_rows():
    waves = WAVE * SP
    phase = (np.arange(waves)[:, None] * np.arange(LONS)[None, :]) % LONS
    phase = phase * (2.0 * math.pi / LONS)
    table = np.stack([np.cos(phase), -np.sin(phase)], axis=1) / math.sqrt(waves)
    return table.reshape(MC, LONS).astype(np.float32)


def dot(a, b, ca, cb):
    return lax.dot_general(a, b, (((ca,), (cb,)), ((), ())), preferred_element_type=F32)


def column(row_ref):
    return jnp.broadcast_to(row_ref[...], (128, row_ref.shape[1])).T


def gelu_pair(v):
    square = v * v
    tanh_part = jnp.tanh(v * (0.7978845608 + 0.7978845608 * 0.044715 * square))
    up = 0.5 + 0.5 * tanh_part
    value = v * up
    bend = 0.7978845608 + 0.7978845608 * 0.134145 * square
    slope = up + 0.5 * v * (1.0 - tanh_part * tanh_part) * bend
    return value, slope


def legendre_back(back, leg):
    wide = back.astype(F32)
    real = wide[:, :LATS].reshape(LATS * SP, CHAN)
    imag = wide[:, LATS:].reshape(LATS * SP, CHAN)
    sums = dot(jnp.concatenate([real, imag], axis=1).astype(BF16), leg, 0, 1)
    return jnp.concatenate([sums[:CHAN], sums[CHAN:]], axis=1)


def sum_of(ref, count):
    first = ref[0].astype(F32)
    whole = lax.fori_loop(1, count, lambda i, t: t + ref[i].astype(F32), first)
    return whole.astype(BF16)


def kernel(
    cot_hbm, grid_hbm, leg_hbm, inv_hbm, gw_hbm, w_in_hbm, b_in_hbm, w_mid_hbm, b_mid_hbm, w_out_hbm,
    tab_hbm, done_hbm, spec_hbm, back_hbm, total_hbm,
    cot, grid, leg, inv, gw, w_in, b_in, w_mid, b_mid, w_out, tab,
    spec, solve, send1, recv1, send2, recv2, wide,
    h_in, h_mid, s_in, s_mid, w_in_t, w_mid_t, col_g, col_in, col_mid,
    acc, acc_bin, acc_bmid, parts, got_a, got_z, summed,
    in_sem, out_sem, own_sem, sum_sem, ready,
    s1_sem, r1_sem, s2_sem, r2_sem, sa_sem, ra_sem, sz_sem, rz_sem, sc_sem, rc_sem,
):
    me = lax.axis_index("space")
    bat = lax.axis_index("batch")
    z, x = lax.div(me, X), lax.rem(me, X)
    gi = bat * X + x

    loads = [
        pltpu.make_async_copy(source, target, in_sem.at[i])
        for i, (source, target) in enumerate([
            (inv_hbm, inv), (cot_hbm.at[0], cot.at[0]), (leg_hbm, leg), (gw_hbm, gw),
            (cot_hbm.at[1], cot.at[1]), (w_in_hbm, w_in), (b_in_hbm, b_in), (w_mid_hbm, w_mid),
            (b_mid_hbm, b_mid), (grid_hbm, grid), (w_out_hbm, w_out), (tab_hbm, tab),
        ])
    ]
    for load in loads[:4]:
        load.start()

    def shift(t):
        i, g = lax.rem(t, 8), lax.div(t, 8)
        return 4 + (1 - 2 * lax.rem(i, 2)) * lax.div(i + 1, 2), g + lax.div(i, 2)

    def space_peer(t):
        dz, dx = shift(t)
        return lax.rem(z + dz, Z) * X + lax.rem(x + dx, X)

    def group_peer(s):
        g = lax.rem(gi + s, 32)
        return g, (z * X + lax.rem(g, X), lax.div(g, X))

    def depth_peer(s):
        return lax.rem(z + s, Z) * X + x

    def each(first, last, act, unroll=1):
        def body(s, carry):
            act(s)
            return carry

        lax.fori_loop(first, last, body, 0, unroll=unroll)

    def peers(act, first=0, last=31):
        each(first, last, lambda t: act(t + lax.div(t + 17, 32)))

    barrier = pltpu.get_barrier_semaphore()

    def greet(t):
        pl.semaphore_signal(barrier, inc=1, device_id=(space_peer(t), bat), device_id_type=MESH)

    def greet_batch(s):
        where = (me, lax.rem(bat + s, NB))
        pl.semaphore_signal(barrier, inc=1, device_id=where, device_id_type=MESH)

    def confirm(s):
        where = (z * X + lax.rem(x + s, X), bat)
        pl.semaphore_signal(ready, inc=1, device_id=where, device_id_type=MESH)

    peers(greet)
    each(1, NB, greet_batch)

    def copy1(b, s):
        peer = space_peer(s)
        return pltpu.make_async_remote_copy(
            src_ref=send1.at[b, peer], dst_ref=recv1.at[b, me],
            send_sem=s1_sem.at[b], recv_sem=r1_sem.at[b],
            device_id=(peer, bat), device_id_type=MESH,
        )

    def copy2(b, s):
        peer = space_peer(s)
        return pltpu.make_async_remote_copy(
            src_ref=send2.at[b, peer], dst_ref=recv2.at[me] if b == 0 else back_hbm.at[me],
            send_sem=s2_sem.at[b], recv_sem=r2_sem.at[b],
            device_id=(peer, bat), device_id_type=MESH,
        )

    def copy_a(s):
        g, where = group_peer(s)
        return pltpu.make_async_remote_copy(
            src_ref=parts.at[pl.ds(pl.multiple_of(g * SEG, SEG), SEG)], dst_ref=got_a.at[gi],
            send_sem=sa_sem, recv_sem=ra_sem, device_id=where, device_id_type=MESH,
        )

    def copy_z(s):
        return pltpu.make_async_remote_copy(
            src_ref=got_z.at[z], dst_ref=got_z.at[z],
            send_sem=sz_sem, recv_sem=rz_sem,
            device_id=(depth_peer(s), bat), device_id_type=MESH,
        )

    def copy_c(s):
        _, where = group_peer(s)
        mine = pl.ds(pl.multiple_of(gi * SEG, SEG), SEG)
        return pltpu.make_async_remote_copy(
            src_ref=summed, dst_ref=total_hbm.at[mine],
            send_sem=sc_sem, recv_sem=rc_sem, device_id=where, device_id_type=MESH,
        )

    def bulk(source, target, send_sem, recv_sem):
        return pltpu.make_async_remote_copy(
            src_ref=source, dst_ref=target, send_sem=send_sem, recv_sem=recv_sem,
            device_id=(space_peer(0), bat), device_id_type=MESH,
        )

    def all1(b):
        part = pl.ds(0, SP - 1)
        return bulk(send1.at[b, part], recv1.at[b, part], s1_sem.at[b], r1_sem.at[b])

    def all2(b):
        part = pl.ds(0, SP - 1)
        target = recv2.at[part] if b == 0 else back_hbm.at[part]
        return bulk(send2.at[b, part], target, s2_sem.at[b], r2_sem.at[b])

    def all_a():
        return bulk(parts.at[pl.ds(0, 31 * SEG)], got_a.at[pl.ds(0, 31)], sa_sem, ra_sem)

    def all_z():
        return bulk(got_z.at[pl.ds(0, Z - 1)], got_z.at[pl.ds(0, Z - 1)], sz_sem, rz_sem)

    def all_c():
        part = pl.ds(0, 31 * SEG)
        return bulk(parts.at[part], total_hbm.at[part], sc_sem, rc_sem)

    lane = lax.broadcasted_iota(jnp.int32, (32, CHAN), 1)
    row = lax.broadcasted_iota(jnp.int32, (32, CHAN), 0)
    repeat = jnp.where(lane % 32 == row, 1.0, 0.0).astype(BF16)
    lane = lax.broadcasted_iota(jnp.int32, (CHAN, CHAN), 1)
    row = lax.broadcasted_iota(jnp.int32, (CHAN, CHAN), 0)
    same = lane // 32 == row // 32

    def spectral_in(b, m):
        if b == 0:
            block = inv[m].reshape(CHAN, 32)
            high = block.astype(BF16)
            low = (block - high.astype(F32)).astype(BF16)
            high = jnp.where(same, dot(high, repeat, 1, 0), 0.0).T.astype(BF16)
            low = jnp.where(same, dot(low, repeat, 1, 0), 0.0).T.astype(BF16)
            solve[m] = jnp.concatenate([high, low, high], axis=1)
        value = cot[b, m]
        value_high = value.astype(BF16)
        value_low = (value - value_high.astype(F32)).astype(BF16)
        grad = dot(
            solve[m], jnp.concatenate([value_high, value_high, value_low], axis=0), 1, 0
        )
        spec[b, m] = grad
        half = grad.astype(BF16)
        half = jnp.concatenate([half[:, :DEG], half[:, DEG:]], axis=0)
        sums = dot(leg[m], half, 0, 1)
        scaled = (sums * jnp.concatenate([col_g[...]] * 2, axis=1)).reshape(SP, LATS, 2 * CHAN)
        scaled = jnp.concatenate([scaled[:, :, :CHAN], scaled[:, :, CHAN:]], axis=1)
        send1[b, :, m] = scaled.astype(BF16)
        if b == 1:
            pltpu.make_async_copy(spec.at[1, m], spec_hbm.at[m], out_sem.at[1, m]).start()

    for load in loads[:4]:
        load.wait()
    for load in loads[4:]:
        load.start()
    col_g[...] = column(gw)
    for b in range(TRAJ):
        if b == 1:
            loads[4].wait()
        for m in range(WAVE):
            spectral_in(b, m)
        if b == 0:
            pl.semaphore_wait(barrier, SP - 1 + NB - 1)
        if b == 0:
            peers(lambda t: copy1(0, t).start())
            each(1, X, confirm)
        recv1[b, me] = send1[b, me]

    for load in loads[5:]:
        load.wait()
    w_in_t[...] = w_in[...].T
    w_mid_t[...] = w_mid[...].T
    col_in[...] = column(b_in)
    col_mid[...] = column(b_mid)
    acc[...] = jnp.zeros_like(acc)
    acc_bin[...] = jnp.zeros_like(acc_bin)
    acc_bmid[...] = jnp.zeros_like(acc_bmid)
    def forward(i):
        b, a = i // LATS, i % LATS
        first = jnp.minimum(4 * i, 31)
        peers(lambda t: copy1(1, t).start(), first, jnp.minimum(first + 4, 31))
        pre = dot(w_in_t[...], grid[b, a], 1, 0)
        value, slope = gelu_pair(pre + jnp.concatenate([col_in[...]] * 4, axis=1))
        hidden = value.astype(BF16)
        h_in[i] = hidden
        s_in[i] = slope
        pre = dot(w_mid_t[...], hidden, 1, 0)
        value, slope = gelu_pair(pre + jnp.concatenate([col_mid[...]] * 4, axis=1))
        h_mid[i] = value.astype(BF16)
        s_mid[i] = slope

    each(0, TRAJ * LATS, forward)

    def lane_sum(v):
        return v[:, :128] + v[:, 128:256] + v[:, 256:384] + v[:, 384:]

    def backward(b, a):
        i = b * LATS + a
        part = wide[pl.ds(a, MC, stride=LATS), :].astype(BF16)
        tend = dot(part, tab[...], 0, 0).astype(BF16)
        acc[768:1024] += dot(h_mid[i], tend, 1, 1)
        err_mid = (dot(w_out[...], tend, 1, 0) * s_mid[i]).astype(BF16)
        mid = dot(h_in[i], err_mid, 1, 1)
        acc[256:512] += mid[:, :128]
        acc[512:768] += mid[:, 128:]
        acc_bmid[...] += lane_sum(err_mid.astype(F32))
        err_in = (dot(w_mid[...], err_mid, 1, 0) * s_in[i]).astype(BF16)
        raw = dot(grid[b, a], err_in, 1, 1)
        acc[0:128] += raw[:, :128]
        acc[128:256] += raw[:, 128:]
        acc_bin[...] += lane_sum(err_in.astype(F32))
        state = dot(w_in[...], err_in, 1, 0).astype(BF16)
        wide[pl.ds(a, MC, stride=LATS), :] = dot(tab[...], state, 1, 1)

    per_peer = 2 * WAVE * LATS

    def unpack(b, peer):
        rows = pl.ds(pl.multiple_of(peer * per_peer, per_peer), per_peer)
        wide[rows, :] = recv1[b, peer].reshape(per_peer, CHAN).astype(F32)

    def pack(b, peer):
        rows = pl.ds(pl.multiple_of(peer * per_peer, per_peer), per_peer)
        send2[b, peer] = wide[rows, :].astype(BF16).reshape(WAVE, 2 * LATS, CHAN)

    for b in range(TRAJ):
        all1(b).wait_recv()
        each(0, SP, functools.partial(unpack, b), 4)
        each(0, LATS, functools.partial(backward, b), 4)

        def depart(t):
            pack(b, space_peer(t))
            copy2(b, t).start()

        if b == 0:
            peers(depart)
            pack(b, me)
            recv2[me] = send2[b, me]

    bins = jnp.sum(acc_bin[...].T, axis=0, keepdims=True)
    bmids = jnp.sum(acc_bmid[...].T, axis=0, keepdims=True)
    acc[1024:1025] = bins[:, :128]
    acc[1025:1026] = bins[:, 128:]
    acc[1026:1027] = bmids[:, :128]
    acc[1027:1028] = bmids[:, 128:]
    parts[...] = acc[...].astype(BF16)
    pl.semaphore_wait(ready, X - 1)
    each(1, 32, lambda s: copy_a(s).start())
    peers(depart, 0, HELD)
    pack(1, me)
    own = pltpu.make_async_copy(send2.at[1, me], back_hbm.at[me], own_sem)
    own.start()
    mine = pl.ds(pl.multiple_of(gi * SEG, SEG), SEG)
    got_a[gi] = parts[mine]
    all_a().wait_recv()
    got_z[z] = sum_of(got_a, 32)
    each(1, Z, lambda s: copy_z(s).start())
    peers(depart, HELD, 31)

    def finish(m):
        spec[0, m] += legendre_back(recv2[:, m], leg[m])
        pltpu.make_async_copy(spec.at[0, m], done_hbm.at[m], out_sem.at[0, m]).start()

    all_z().wait_recv()
    summed[...] = sum_of(got_z, Z)
    own_sum = pltpu.make_async_copy(summed, total_hbm.at[mine], sum_sem)
    own_sum.start()
    each(1, 32, lambda s: copy_c(s).start())
    all2(0).wait_recv()
    for m in range(WAVE):
        finish(m)
    own.wait()
    own_sum.wait()
    for b in range(TRAJ):
        all1(b).wait_send()
        all2(b).wait_send()
    for m in range(WAVE):
        pltpu.make_async_copy(spec.at[0, m], done_hbm.at[m], out_sem.at[0, m]).wait()
        pltpu.make_async_copy(spec.at[1, m], spec_hbm.at[m], out_sem.at[1, m]).wait()
    all_a().wait_send()
    all_z().wait_send()
    all_c().wait_recv()
    all_c().wait_send()
    all2(1).wait_recv()


def last_kernel(
    done_hbm, spec_hbm, back_hbm, leg_hbm, total_hbm,
    out_hbm, in_hbm, bin_hbm, mid_hbm, bmid_hbm, wout_hbm,
    g_in, g_bin, g_mid, g_bmid, g_out, held, spec, back, leg, total,
    sem, out_sem, done_sem, total_sem, grad_sem,
):
    done = pltpu.make_async_copy(done_hbm, held, done_sem.at[0])
    stores = [pltpu.make_async_copy(held, out_hbm.at[0], done_sem.at[1])]
    loads = [
        [
            pltpu.make_async_copy(back_hbm.at[:, m], back.at[:, m], sem.at[m, 0]),
            pltpu.make_async_copy(leg_hbm.at[m], leg.at[m], sem.at[m, 1]),
            pltpu.make_async_copy(spec_hbm.at[m], spec.at[m], sem.at[m, 2]),
        ]
        for m in range(WAVE)
    ]
    sums = pltpu.make_async_copy(total_hbm, total, total_sem)
    sums.start()
    for load in sum(loads, []):
        load.start()
    done.start()
    sums.wait()
    whole = total[...].astype(F32)
    squares = whole * whole
    factor = jnp.minimum(F32(1.0), LIMIT / jnp.sqrt(jnp.sum(squares, keepdims=True) + 1e-06))
    g_in[:, :128] = factor * whole[0:128]
    g_in[:, 128:] = factor * whole[128:256]
    g_mid[:, :128] = factor * whole[256:512]
    g_mid[:, 128:] = factor * whole[512:768]
    g_out[...] = factor * whole[768:1024]
    g_bin[:, :128] = factor * whole[1024:1025]
    g_bin[:, 128:] = factor * whole[1025:1026]
    g_bmid[:, :128] = factor * whole[1026:1027]
    g_bmid[:, 128:] = factor * whole[1027:1028]
    for i, (source, target) in enumerate([
        (g_in, in_hbm), (g_bin, bin_hbm), (g_mid, mid_hbm), (g_bmid, bmid_hbm), (g_out, wout_hbm),
    ]):
        stores.append(pltpu.make_async_copy(source, target, grad_sem.at[i]))
        stores[-1].start()
    for m in range(WAVE):
        for load in loads[m]:
            load.wait()
        spec[m] += legendre_back(back[:, m], leg[m])
        stores.append(pltpu.make_async_copy(spec.at[m], out_hbm.at[1, m], out_sem.at[m]))
        stores[-1].start()
        if m == 1:
            done.wait()
            stores[0].start()
    for store in stores:
        store.wait()


def shards(
    cotangent, grid_state, legendre, inverse, gauss_weights, w_in, bias_in, w_mid, bias_mid, w_out
):
    table = jnp.asarray(fourier_rows(), F32).astype(BF16)
    hbm = pl.BlockSpec(memory_space=pl.ANY)
    cols = TRAJ * LATS
    message = (TRAJ, SP, WAVE, 2 * LATS, CHAN)
    dma = pltpu.SemaphoreType.DMA
    state_half = jax.ShapeDtypeStruct((WAVE, CHAN, COEF), F32)
    done, spec, back, total = pl.pallas_call(
        kernel,
        name="exchange",
        out_shape=(
            state_half,
            state_half,
            jax.ShapeDtypeStruct(message[1:], BF16),
            jax.ShapeDtypeStruct((ROWS, 128), BF16),
        ),
        in_specs=[hbm] * 11,
        out_specs=[hbm] * 4,
        scratch_shapes=[
            pltpu.VMEM((TRAJ, WAVE, CHAN, COEF), F32),
            pltpu.VMEM((TRAJ, LATS, CHAN, LONS), BF16),
            pltpu.VMEM((WAVE, DEG, LATS * SP), BF16),
            pltpu.VMEM((WAVE, 4, 32, 32), F32),
            pltpu.VMEM((1, LATS * SP), F32),
            pltpu.VMEM((CHAN, HIDDEN), BF16),
            pltpu.VMEM((1, HIDDEN), F32),
            pltpu.VMEM((HIDDEN, HIDDEN), BF16),
            pltpu.VMEM((1, HIDDEN), F32),
            pltpu.VMEM((HIDDEN, CHAN), BF16),
            pltpu.VMEM((MC, LONS), BF16),
            pltpu.VMEM((TRAJ, WAVE, CHAN, COEF), F32),
            pltpu.VMEM((WAVE, CHAN, 3 * CHAN), BF16),
            pltpu.VMEM(message, BF16),
            pltpu.VMEM(message, BF16),
            pltpu.VMEM(message, BF16),
            pltpu.VMEM(message[1:], BF16),
            pltpu.VMEM((MC * LATS, CHAN), F32),
            pltpu.VMEM((cols, HIDDEN, LONS), BF16),
            pltpu.VMEM((cols, HIDDEN, LONS), BF16),
            pltpu.VMEM((cols, HIDDEN, LONS), F32),
            pltpu.VMEM((cols, HIDDEN, LONS), F32),
            pltpu.VMEM((HIDDEN, CHAN), BF16),
            pltpu.VMEM((HIDDEN, HIDDEN), BF16),
            pltpu.VMEM((LATS * SP, 128), F32),
            pltpu.VMEM((HIDDEN, 128), F32),
            pltpu.VMEM((HIDDEN, 128), F32),
            pltpu.VMEM((ROWS, 128), F32),
            pltpu.VMEM((HIDDEN, 128), F32),
            pltpu.VMEM((HIDDEN, 128), F32),
            pltpu.VMEM((ROWS, 128), BF16),
            pltpu.VMEM((32, SEG, 128), BF16),
            pltpu.VMEM((Z, SEG, 128), BF16),
            pltpu.VMEM((SEG, 128), BF16),
            dma((12,)),
            dma((TRAJ, WAVE)),
            dma,
            dma,
            pltpu.SemaphoreType.REGULAR,
            dma((TRAJ,)),
            dma((TRAJ,)),
            dma((TRAJ,)),
            dma((TRAJ,)),
            dma,
            dma,
            dma,
            dma,
            dma,
            dma,
        ],
        compiler_params=pltpu.CompilerParams(
            collective_id=0, has_side_effects=True, vmem_limit_bytes=60 * 1024 * 1024
        ),
    )(
        cotangent, grid_state, legendre, inverse, gauss_weights.reshape(1, -1),
        w_in, bias_in.reshape(1, -1), w_mid, bias_mid.reshape(1, -1), w_out, table,
    )
    state, g_in, g_bin, g_mid, g_bmid, g_out = pl.pallas_call(
        last_kernel,
        name="finish",
        out_shape=(
            jax.ShapeDtypeStruct((TRAJ, WAVE, CHAN, COEF), F32),
            jax.ShapeDtypeStruct((CHAN, HIDDEN), F32),
            jax.ShapeDtypeStruct((1, HIDDEN), F32),
            jax.ShapeDtypeStruct((HIDDEN, HIDDEN), F32),
            jax.ShapeDtypeStruct((1, HIDDEN), F32),
            jax.ShapeDtypeStruct((HIDDEN, CHAN), F32),
        ),
        in_specs=[hbm] * 5,
        out_specs=[hbm] * 6,
        scratch_shapes=[
            pltpu.VMEM((CHAN, HIDDEN), F32),
            pltpu.VMEM((1, HIDDEN), F32),
            pltpu.VMEM((HIDDEN, HIDDEN), F32),
            pltpu.VMEM((1, HIDDEN), F32),
            pltpu.VMEM((HIDDEN, CHAN), F32),
            pltpu.VMEM((WAVE, CHAN, COEF), F32),
            pltpu.VMEM((WAVE, CHAN, COEF), F32),
            pltpu.VMEM(message[1:], BF16),
            pltpu.VMEM((WAVE, DEG, LATS * SP), BF16),
            pltpu.VMEM((ROWS, 128), BF16),
            dma((WAVE, 3)),
            dma((WAVE,)),
            dma((2,)),
            dma,
            dma((5,)),
        ],
        compiler_params=pltpu.CompilerParams(vmem_limit_bytes=60 * 1024 * 1024),
    )(done, spec, back, legendre, total)
    return state, g_in, g_bin.reshape(-1), g_mid, g_bmid.reshape(-1), g_out


def solution(mesh):
    return jax.shard_map(
        shards,
        mesh=mesh,
        in_specs=(
            P("batch", "space", None, None),
            P("batch", "space", None, None),
            P("space", None, None),
            P("space", None, None, None),
            P(),
            P(),
            P(),
            P(),
            P(),
            P(),
        ),
        out_specs=(P("batch", "space", None, None), P(), P(), P(), P(), P()),
        check_vma=False,
    )
```
